512 devices in a mesh: dp: 64 (over z, x, core), tensor: 8 (over y).
Axes of the slice: x: 4, y: 8, z: 8, core: 2. Of those that a mesh axis runs over, the one named last changes fastest.
Arguments:
- acts: bfloat16 [16384, 8192], P('dp', 'tensor'), may hold values from -6 to 6
- mean_vec: float32 [8192], P('tensor'), may hold values from -3 to 3
- left_factor: bfloat16 [512, 8192], P('dp', 'tensor'), may hold values from -0.25 to 0.25
- right_factor: bfloat16 [512, 8192], P('dp', 'tensor'), may hold values from -0.0625 to 0.0625
- labels: int32 [16384], P('dp'), may hold values from 0 to 511, as said below
- counts: int32 [64], P('dp'), may hold values from 69 to 256, as said below
Outputs:
- erased: bfloat16 [16384, 8192], P('dp', 'tensor')
- class_scores: float32 [512, 8192], P('dp', 'tensor')
- class_counts: int32 [512], P('dp')
The draws below stay inside these ranges and needn't reach their ends.
Inputs may be any that keep to these rules, and one draw needn't show every extreme that they name: `counts`: some data shard is full. `labels`: class frequencies are skewed; at least two classes occur in no token slot.
All inputs are finite; a program needn't handle non-finite values.
Results may differ from the reference program's by a relative error of at most 0.0053.
Values may be sent and summed in bfloat16 or wider, within the bound.
A program may use at most 64 MiB of HBM per device.

```python
import jax
import jax.numpy as jnp
from jax import lax

D = 8192
C = 512
R = 512
TOK_DEV = 256
SHARDS = 64
TOKENS = 16384


def draw_counts(key, part):
    key = jax.random.fold_in(key, 7)
    shard_ids = jnp.arange(SHARDS, dtype=jnp.int32)
    lowest = TOK_DEV // 3
    rising = lowest + shard_ids * (TOK_DEV - lowest) // max(SHARDS - 1, 1)
    jitter = jax.random.randint(key, (SHARDS,), 0, TOK_DEV // 16 + 1, dtype=jnp.int32)
    values = jnp.minimum(rising - jitter, TOK_DEV)
    return values.at[SHARDS - 1].set(TOK_DEV)


def draw_labels(key, part):
    key = jax.random.fold_in(key, 11)
    key_one, key_two, key_three, key_order = jax.random.split(key, 4)
    first = jax.random.randint(key_one, (TOKENS,), 0, C, dtype=jnp.int32)
    second = jax.random.randint(key_two, (TOKENS,), 0, C, dtype=jnp.int32)
    third = jax.random.randint(key_three, (TOKENS,), 0, C, dtype=jnp.int32)
    ranks = first * second * third // (C * C)
    ranks = jnp.minimum(ranks, C - 3)
    order = jax.random.permutation(key_order, jnp.arange(C, dtype=jnp.int32))
    return jnp.take(order, ranks).astype(jnp.int32)


def level_of(stream_key, shape, cuts, low, largest):
    level = 1.0
    for axis_at, blocks in cuts:
        heights = jax.random.uniform(jax.random.fold_in(jax.random.fold_in(stream_key, 6), axis_at), (blocks,), jnp.float32, low / len(cuts), largest / len(cuts))
        level = level * jnp.repeat(jnp.exp(heights), shape[axis_at] // blocks).reshape((-1,) + (1,) * (len(shape) - 1 - axis_at))
    return level


def gaussian(own_key, shape, width, reach, cuts=(), kind=jnp.bfloat16):
    drawn = width * jax.random.normal(own_key, shape, jnp.float32)
    if cuts:
        drawn = drawn * level_of(own_key, shape, cuts, -0.22, 0.18)
    return jnp.clip(drawn, -reach, reach).astype(kind)


def setup_inputs(seed: int = 0) -> dict:
    keys = jax.random.split(jax.random.key(seed), 7)
    acts = gaussian(keys[0], (TOKENS, D), 1.0, 6.0, ((0, 64), (1, 8)))
    mean_vec = gaussian(keys[1], (D,), 0.5, 3.0, ((0, 8),), jnp.float32)
    left_factor = gaussian(keys[2], (R, D), R ** -0.5, 0.25, ((0, 64), (1, 8)))
    right_factor = gaussian(keys[3], (R, D), D ** -0.5, 0.0625, ((0, 64), (1, 8)))
    labels = draw_labels(jax.random.fold_in(keys[6], 71), 0)
    counts = draw_counts(jax.random.fold_in(keys[6], 71), 0)
    return dict(acts=acts, mean_vec=mean_vec, left_factor=left_factor, right_factor=right_factor, labels=labels, counts=counts)


def reference(acts, mean_vec, left_factor, right_factor, labels, counts):
    blocks = acts.reshape(SHARDS, TOK_DEV, D)
    label_blocks = labels.reshape(SHARDS, TOK_DEV)

    def shard_step(running, shard_item):
        class_total, count_total, feature_total = running
        block, label_row, valid_count = shard_item
        centred = (block.astype(jnp.float32) - mean_vec[None, :]).astype(jnp.bfloat16)
        coords = jnp.dot(centred, right_factor.T, preferred_element_type=jnp.float32).astype(jnp.bfloat16)
        correction = jnp.dot(coords, left_factor, preferred_element_type=jnp.float32)
        erased_block = (block.astype(jnp.float32) - correction).astype(jnp.bfloat16)
        valid_rows = jnp.arange(TOK_DEV, dtype=jnp.int32) < valid_count
        label_hits = (label_row[:, None] == jnp.arange(C, dtype=jnp.int32)[None, :]) & valid_rows[:, None]
        onehot = label_hits.astype(jnp.bfloat16)
        class_total = class_total + jnp.dot(onehot.T, erased_block, preferred_element_type=jnp.float32)
        count_total = count_total + lax.optimization_barrier(jnp.sum(label_hits.astype(jnp.float32), axis=0))
        feature_total = feature_total + jnp.dot(valid_rows.astype(jnp.bfloat16), erased_block, preferred_element_type=jnp.float32)
        return ((class_total, count_total, feature_total), erased_block)
    start_state = (jnp.zeros((C, D), jnp.float32), jnp.zeros((C,), jnp.float32), jnp.zeros((D,), jnp.float32))
    final_state, erased_blocks = lax.scan(shard_step, start_state, (blocks, label_blocks, counts))
    class_total, count_total, feature_total = final_state
    grand_total = jnp.sum(count_total)
    feature_mean = feature_total / grand_total
    scale_rows = 1.0 / jnp.sqrt(jnp.maximum(count_total, 1.0))
    class_scores = (class_total - count_total[:, None] * feature_mean[None, :]) * scale_rows[:, None]
    return (erased_blocks.reshape(TOKENS, D), class_scores, count_total.astype(jnp.int32))
```

```python
import functools

import jax
import jax.numpy as jnp
from jax import lax
from jax.experimental import pallas as pl
from jax.experimental.pallas import tpu as pltpu
from jax.sharding import PartitionSpec as P

MESH = pl.DeviceIdType.MESH
F32, BF16 = jnp.float32, jnp.bfloat16
C = 512
NZ, NX, NY = 8, 4, 8
ZORD = (0, 1, 7, 2, 6, 3, 5, 4)
XORD = (0, 1, 3, 2)
ZPOS = {d: s for s, d in enumerate(ZORD)}
XPOS = {d: s for s, d in enumerate(XORD)}
FAR = (7, 6, 5, 4, 3, 2, 1)
GROUPS = ((0, 2), (2, 2), (4, 2), (6, 2))
TOK, D, RD = 256, 1024, 8
T2, H, K2 = 512, 512, 128
QN = 2
QW = H // QN
YB = T2 // NY


def kernel(
    acts, mean, left, right, labels, counts,
    out, scores, cnt,
    actv, cen, rg, lg, lm, lab, pbuf, prx, cbuf, oh, er,
    sxs, sxr, s0, txs, txr, szs, szr, tzs, tzr,
    loc, rzs, rzr, rxs, rxr, lzs, lzr, lxs, lxr, bzs, bzr, bxs, bxr, exs, exr,
    pss, psr, css, csr, xxs, xxr, zzs, zzr,
):
    dp, y = lax.axis_index("dp"), lax.axis_index("tensor")
    c, x, z = lax.rem(dp, 2), lax.rem(dp // 2, NX), dp // (2 * NX)
    oc = 1 - c

    def dev(dz=0, dx=0, core=None, dy=0):
        core = c if core is None else core
        zz, xx, yy = lax.rem(z + dz, NZ), lax.rem(x + dx, NX), lax.rem(y + dy, NY)
        return ((zz * NX + xx) * 2 + core, yy)

    sent = []

    def send(src, dst, ss, rs, to):
        cp = pltpu.make_async_remote_copy(
            src_ref=src, dst_ref=dst, send_sem=ss, recv_sem=rs, device_id=to, device_id_type=MESH
        )
        cp.start()
        sent.append(cp)

    def got(dst, rs):
        pltpu.make_async_remote_copy(
            src_ref=dst, dst_ref=dst, send_sem=rs, recv_sem=rs, device_id=dev(core=oc), device_id_type=MESH
        ).wait_recv()

    mine = pl.ds(pl.multiple_of(c * TOK, TOK), TOK)
    theirs = pl.ds(pl.multiple_of(oc * TOK, TOK), TOK)
    loads = [
        pltpu.make_async_copy(right, rg.at[0, 0], loc.at[0]),
        pltpu.make_async_copy(acts, actv.at[mine], loc.at[1]),
    ]
    for cp in loads:
        cp.start()

    barrier = pltpu.get_barrier_semaphore()
    peers = [dev(dz=d, core=k) for d in range(1, NZ) for k in (c, oc)]
    peers += [dev(dx=d) for d in range(1, NX)] + [dev(dy=d) for d in range(1, NY)] + [dev(core=oc)]
    for p in peers:
        pl.semaphore_signal(barrier, inc=1, device_id=p, device_id_type=MESH)
    slot_iota = lax.broadcasted_iota(jnp.int32, (1, TOK), 1)
    lab[c, 0, 0] = jnp.where(slot_iota < counts[0], labels[...], -1)
    loads[0].wait()
    loads[1].wait()
    pl.semaphore_wait(barrier, len(peers))

    for s in FAR:
        d = ZORD[s]
        t = ZPOS[(NZ - d) % NZ]
        send(rg.at[0, 0], rg.at[0, t], rzs.at[s], rzr.at[t], dev(dz=d))
    send(actv.at[mine], actv.at[mine], exs.at[0], exr.at[0], dev(core=oc))
    for s in FAR:
        d = ZORD[s]
        t = ZPOS[(NZ - d) % NZ]
        send(lab.at[c, 0, 0], lab.at[c, 0, t], bzs.at[s], bzr.at[t], dev(dz=d))
    for s in FAR:
        d = ZORD[s]
        t = ZPOS[(NZ - d) % NZ]
        for k, core in enumerate((c, oc)):
            cols = pl.ds(pl.multiple_of(core * H, H), H)
            send(left.at[:, cols], lg.at[c, 0, t], lzs.at[k, s], lzr.at[k, t], dev(dz=d, core=core))
    send(left.at[:, pl.ds(pl.multiple_of(oc * H, H), H)], lg.at[c, 0, 0], lzs.at[1, 0], lzr.at[1, 0], dev(core=oc))
    lg[c, 0, 0] = left[:, pl.ds(pl.multiple_of(c * H, H), H)]

    cen[mine, :] = (actv[mine, :].astype(F32) - mean[...]).astype(BF16)

    for g, (first, number) in enumerate(GROUPS):
        for s in range(first, first + number):
            if s:
                got(rg.at[0, s], rzr.at[s])
        for s in (3, 2, 1):
            d = XORD[s]
            t = XPOS[(NX - d) % NX]
            zs = pl.ds(first, number)
            send(rg.at[0, zs], rg.at[t, zs], rxs.at[s, g], rxr.at[t, g], dev(dx=d))
    got(actv.at[theirs], exr.at[0])
    cen[theirs, :] = (actv[theirs, :].astype(F32) - mean[...]).astype(BF16)

    for s in range(1, NZ):
        got(lab.at[c, 0, s], bzr.at[s])
    for s in (3, 2, 1):
        d = XORD[s]
        t = XPOS[(NX - d) % NX]
        send(lab.at[c, 0], lab.at[c, t], bxs.at[s], bxr.at[t], dev(dx=d))

    def chunk(k):
        for xs in (2 * k, 2 * k + 1):
            for g, (first, number) in enumerate(GROUPS):
                if xs:
                    zs = pl.ds(first, number)
                    got(rg.at[xs, zs], rxr.at[xs, g])
        rmat = rg[2 * k : 2 * k + 2].astype(F32).reshape(K2, D).astype(BF16)
        part = lax.dot_general(cen[...], rmat, (((1,), (1,)), ((), ())), preferred_element_type=F32)
        pbuf[k] = part.astype(BF16)
        for s in FAR:
            d = ZORD[s]
            t = ZPOS[(NY - d) % NY]
            rows = pl.ds(pl.multiple_of(lax.rem(y + d, NY) * YB, YB), YB)
            send(pbuf.at[k, rows], prx.at[k, t], pss.at[k, s], psr.at[k, t], dev(dy=d))

    own_rows = pl.ds(pl.multiple_of(y * YB, YB), YB)

    def reduce(k):
        total = pbuf[k, own_rows, :].astype(F32)
        for s in range(1, NY):
            got(prx.at[k, s], psr.at[k, s])
            total = total + prx[k, s].astype(F32)
        cbuf[c, k, own_rows, :] = total.astype(BF16)
        for s in FAR:
            d = ZORD[s]
            t = ZPOS[(NY - d) % NY]
            send(cbuf.at[c, k, own_rows], cbuf.at[c, k, own_rows], css.at[k, s], csr.at[k, t], dev(dy=d))

    def gathered(k):
        for s in range(1, NY):
            rows = pl.ds(pl.multiple_of(lax.rem(y + ZORD[s], NY) * YB, YB), YB)
            got(cbuf.at[c, k, rows], csr.at[k, s])
        send(cbuf.at[c, k], cbuf.at[c, k], exs.at[2 + k], exr.at[2 + k], dev(core=oc))

    chunk(0)
    got(lg.at[oc, 0, 0], lzr.at[1, 0])
    for s in range(1, NZ):
        got(lg.at[c, 0, s], lzr.at[0, s])
        got(lg.at[oc, 0, s], lzr.at[1, s])
    for s in (3, 2, 1):
        d = XORD[s]
        t = XPOS[(NX - d) % NX]
        send(lg.at[:, 0], lg.at[:, t], lxs.at[s], lxr.at[t], dev(dx=d))
    chunk(1)

    for s in range(1, NX):
        got(lab.at[c, s], bxr.at[s])
    send(lab.at[c], lab.at[c], exs.at[1], exr.at[1], dev(core=oc))
    got(lab.at[oc], exr.at[1])
    own_class = dp * RD + lax.broadcasted_iota(jnp.int32, (RD, TOK), 0)
    hits, valid = jnp.zeros((RD, TOK), F32), jnp.zeros((1, TOK), F32)
    for k in range(2):
        for xs in range(NX):
            for zs in range(NZ):
                row = lab[k, xs, zs]
                hits = hits + (row == own_class).astype(F32)
                valid = valid + (row >= 0).astype(F32)
    own_counts = jnp.sum(hits, axis=1, keepdims=True)
    grand = jnp.sum(valid, axis=1, keepdims=True)
    tokens = jnp.concatenate([lab[0, 0, 0], lab[1, 0, 0]], axis=1)
    for xs in range(NX):
        for zs in range(NZ):
            r = lax.broadcasted_iota(jnp.int32, (2 * RD, T2), 0)
            owner = lax.rem(z + ZORD[zs], NZ) * NX + lax.rem(x + XORD[xs], NX)
            at = (xs * NZ + zs) * 2 * RD
            oh[at : at + 2 * RD, :] = (owner * (2 * RD) + r == tokens).astype(F32).astype(BF16)

    reduce(0)
    for s in range(1, NX):
        got(lg.at[:, s], lxr.at[s])
    for k in range(2):
        lm[k * 256 : (k + 1) * 256, :] = lg[k].astype(F32).reshape(256, H).astype(BF16)
    reduce(1)
    gathered(0)
    gathered(1)
    for k in range(2):
        got(cbuf.at[oc, k], exr.at[2 + k])

    coords = jnp.concatenate([cbuf[0, 0], cbuf[0, 1], cbuf[1, 0], cbuf[1, 1]], axis=1)
    for q in range(QN):
        cols = slice(q * QW, (q + 1) * QW)
        corr = jnp.dot(coords, lm[:, cols], preferred_element_type=F32)
        acols = pl.ds(pl.multiple_of(c * H + q * QW, QW), QW)
        er[:, cols] = (actv[:, acols].astype(F32) - corr).astype(BF16)
        sums = jnp.dot(oh[...], er[:, cols], preferred_element_type=F32)
        s0[:, cols] = sums[:128]
        txs[:, cols] = jnp.sum(sums, axis=0, keepdims=True)
        for s in (3, 2, 1):
            d = XORD[s]
            t = XPOS[(NX - d) % NX]
            sxs[q, s] = sums[s * 128 : (s + 1) * 128].astype(BF16)
            send(sxs.at[q, s], sxr.at[q, t], xxs.at[q, s], xxr.at[q, t], dev(dx=d))
    for s in (3, 2, 1):
        d = XORD[s]
        t = XPOS[(NX - d) % NX]
        send(txs, txr.at[t], xxs.at[QN, s], xxr.at[QN, t], dev(dx=d))
    half = pl.ds(pl.multiple_of(c * H, H), H)
    keep = pltpu.make_async_copy(er.at[mine], out.at[:, half], loc.at[2])
    keep.start()
    send(er.at[theirs], out.at[:, half], exs.at[4], exr.at[4], dev(core=oc))

    for q in range(QN):
        cols = slice(q * QW, (q + 1) * QW)
        total = s0[:, cols]
        for s in range(1, NX):
            got(sxr.at[q, s], xxr.at[q, s])
            total = total + sxr[q, s].astype(F32)
        s0[:, cols] = total
    tot = txs[...]
    for s in range(1, NX):
        got(txr.at[s], xxr.at[QN, s])
        tot = tot + txr[s]
    tzs[...] = tot

    for s in FAR + (0,):
        d = ZORD[s]
        t = ZPOS[(NZ - d) % NZ]
        for core in range(2):
            at = (s * 2 + core) * RD
            szs[s, core] = s0[at : at + RD, :].astype(BF16)
        for k, core in enumerate((c, oc)):
            if s == 0 and k == 0:
                continue
            send(szs.at[s, core], szr.at[c, t], zzs.at[0, k, s], zzr.at[0, k, t], dev(dz=d, core=core))
            send(tzs, tzr.at[c, t], zzs.at[1, k, s], zzr.at[1, k, t], dev(dz=d, core=core))
    szr[c, 0] = szs[0, c]
    tzr[c, 0] = tot
    for s in range(NZ):
        for k, core in enumerate((c, oc)):
            if s == 0 and k == 0:
                continue
            got(szr.at[core, s], zzr.at[0, k, s])
            got(tzr.at[core, s], zzr.at[1, k, s])
    scale = 1.0 / jnp.sqrt(jnp.maximum(own_counts, 1.0))
    for h in range(2):
        class_sums, totals = szr[h, 0].astype(F32), tzr[h, 0]
        for s in range(1, NZ):
            class_sums = class_sums + szr[h, s].astype(F32)
            totals = totals + tzr[h, s]
        feature_mean = totals / grand
        scores[:, h * H : (h + 1) * H] = (class_sums - own_counts * feature_mean) * scale
    lane = lax.broadcasted_iota(jnp.int32, (RD, RD), 1)
    row = lax.broadcasted_iota(jnp.int32, (RD, RD), 0)
    cnt[...] = jnp.sum(jnp.where(lane == row, own_counts, 0.0), axis=0, keepdims=True).astype(jnp.int32)

    keep.wait()
    got(out.at[:, pl.ds(pl.multiple_of(oc * H, H), H)], exr.at[4])
    for cp in sent:
        cp.wait_send()


def per_device(acts, mean_vec, left_factor, right_factor, labels, counts):
    dma = pltpu.SemaphoreType.DMA
    ng = len(GROUPS)
    vm, hbm = pl.BlockSpec(memory_space=pltpu.VMEM), pl.BlockSpec(memory_space=pl.ANY)
    erased, scores, cnt = pl.pallas_call(
        kernel,
        out_shape=(
            jax.ShapeDtypeStruct((TOK, D), BF16),
            jax.ShapeDtypeStruct((RD, D), F32),
            jax.ShapeDtypeStruct((1, RD), jnp.int32),
        ),
        in_specs=[hbm, vm, vm, hbm, vm, pl.BlockSpec(memory_space=pltpu.SMEM)],
        out_specs=(hbm, vm, vm),
        scratch_shapes=[
            pltpu.VMEM((T2, D), BF16),
            pltpu.VMEM((T2, D), BF16),
            pltpu.VMEM((NX, NZ, RD, D), BF16),
            pltpu.VMEM((2, NX, NZ, RD, H), BF16),
            pltpu.VMEM((C, H), BF16),
            pltpu.VMEM((2, NX, NZ, 1, TOK), jnp.int32),
            pltpu.VMEM((2, T2, K2), BF16),
            pltpu.VMEM((2, NY, YB, K2), BF16),
            pltpu.VMEM((2, 2, T2, K2), BF16),
            pltpu.VMEM((C, T2), BF16),
            pltpu.VMEM((T2, H), BF16),
            pltpu.VMEM((QN, NX, 128, QW), BF16),
            pltpu.VMEM((QN, NX, 128, QW), BF16),
            pltpu.VMEM((128, H), F32),
            pltpu.VMEM((1, H), F32),
            pltpu.VMEM((NX, 1, H), F32),
            pltpu.VMEM((NZ, 2, RD, H), BF16),
            pltpu.VMEM((2, NZ, RD, H), BF16),
            pltpu.VMEM((1, H), F32),
            pltpu.VMEM((2, NZ, 1, H), F32),
            dma((3,)),
            dma((NZ,)), dma((NZ,)),
            dma((NX, ng)), dma((NX, ng)),
            dma((2, NZ)), dma((2, NZ)),
            dma((NX,)), dma((NX,)),
            dma((NZ,)), dma((NZ,)),
            dma((NX,)), dma((NX,)),
            dma((5,)), dma((5,)),
            dma((2, NY)), dma((2, NY)),
            dma((2, NY)), dma((2, NY)),
            dma((QN + 1, NX)), dma((QN + 1, NX)),
            dma((2, 2, NZ)), dma((2, 2, NZ)),
        ],
        compiler_params=pltpu.CompilerParams(
            collective_id=0, has_side_effects=True, vmem_limit_bytes=40 << 20
        ),
        cost_estimate=pl.CostEstimate(flops=6 * 256 * 1024 * 512, bytes_accessed=4 << 20, transcendentals=0),
    )(
        acts,
        mean_vec.reshape(1, D),
        left_factor,
        right_factor,
        labels.reshape(1, TOK),
        counts,
    )
    return erased, scores, cnt.reshape(RD)


def solution(mesh):
    return jax.shard_map(
        per_device,
        mesh=mesh,
        in_specs=(
            P("dp", "tensor"),
            P("tensor"),
            P("dp", "tensor"),
            P("dp", "tensor"),
            P("dp"),
            P("dp"),
        ),
        out_specs=(P("dp", "tensor"), P("dp", "tensor"), P("dp")),
        check_vma=False,
    )
```

```python
import functools

import jax
import jax.numpy as jnp
from jax import lax
from jax.experimental import pallas as pl
from jax.experimental.pallas import tpu as pltpu
from jax.sharding import PartitionSpec as P

MESH = pl.DeviceIdType.MESH
F32, BF16, I32 = jnp.float32, jnp.bfloat16, jnp.int32
C = 512
NZ, NX, NY = 8, 4, 8
ZORD = (0, 1, 7, 2, 6, 3, 5, 4)
XORD = (0, 1, 3, 2)
ZBACK = tuple(ZORD.index((NZ - d) % NZ) for d in ZORD)
XBACK = tuple(XORD.index((NX - d) % NX) for d in XORD)
NEAR, FAR = (1, 2, 3, 4, 5, 6, 7), (7, 6, 5, 4, 3, 2, 1)
XFIRST = (2, 3, 1)
GROUPS = ((0, 2), (2, 2), (4, 2), (6, 2))
TOK, D, RD = 256, 1024, 8
T2, H, K2 = 512, 512, 128
QN = 2
QW = H // QN
YB = T2 // NY
VLIM = 63 << 20


def kernel(
    acts, mean, left, right, labels, counts,
    out, scores, cnt,
    meanv, labv, cntv, actv, cen, rg, lg, lo, lm, lab, pbuf, prx, cbuf, oh, er,
    sxs, sxr, s0, txs, txr, szs, szr, tzs, tzr, fin,
    loc, rzs, rzr, rxs, rxr, lzs, lzr, lxs, lxr, bzs, bzr, bxs, bxr, exs, exr,
    pss, psr, css, csr, fcs, fcr, xxs, xxr, zzs, zzr,
):
    dp, y = lax.axis_index("dp"), lax.axis_index("tensor")
    c, x, z = lax.rem(dp, 2), lax.rem(dp // 2, NX), dp // (2 * NX)
    oc = 1 - c

    def dev(dz=0, dx=0, dy=0, core=None):
        core = c if core is None else core
        zz, xx, yy = lax.rem(z + dz, NZ), lax.rem(x + dx, NX), lax.rem(y + dy, NY)
        return ((zz * NX + xx) * 2 + core, yy)

    other = dev(core=oc)

    def send(src, dst, ss, rs, to):
        pltpu.make_async_remote_copy(
            src_ref=src,
            dst_ref=dst,
            send_sem=ss[0].at[ss[1]],
            recv_sem=rs[0].at[rs[1]],
            device_id=to,
            device_id_type=MESH,
        ).start()

    def got(ref, rs):
        sem = rs[0].at[rs[1]]
        pltpu.make_async_remote_copy(
            src_ref=ref, dst_ref=ref, send_sem=sem, recv_sem=sem, device_id=other, device_id_type=MESH
        ).wait_recv()

    def gone(ref, ss):
        sem = ss[0].at[ss[1]]
        pltpu.make_async_remote_copy(
            src_ref=ref, dst_ref=ref, send_sem=sem, recv_sem=sem, device_id=other, device_id_type=MESH
        ).wait_send()

    def along_z(order, src, dst, ss, rs):
        for s in order:
            send(src(s), dst(ZBACK[s]), ss, rs(ZBACK[s]), dev(dz=ZORD[s]))

    def along_y(order, src, dst, ss, rs):
        for s in order:
            send(src(s), dst(ZBACK[s]), ss, rs(ZBACK[s]), dev(dy=ZORD[s]))

    def along_x(src, dst, ss, rs):
        for s in XFIRST:
            send(src(s), dst(XBACK[s]), ss, rs(XBACK[s]), dev(dx=XORD[s]))

    mine, theirs = pl.ds(0, TOK), pl.ds(TOK, TOK)
    loads = [
        pltpu.make_async_copy(src, dst, loc.at[i])
        for i, (src, dst) in enumerate(
            (
                (right, rg.at[0, 0]),
                (acts, actv.at[mine]),
                (mean, meanv),
                (labels, labv),
                (counts, cntv),
                (left, lg.at[0, 0]),
            )
        )
    ]
    for cp in loads:
        cp.start()

    barrier = pltpu.get_barrier_semaphore()
    peers = [dev(dz=ZORD[s]) for s in FAR] + [dev(dy=ZORD[s]) for s in FAR]
    peers += [dev(dx=d) for d in (2, 1, 3)] + [other]
    for p in peers:
        pl.semaphore_signal(barrier, inc=1, device_id=p, device_id_type=MESH)
    loads[0].wait()
    pl.semaphore_wait(barrier, len(peers))

    group_of = {s: g for g, (first, number) in enumerate(GROUPS) for s in range(first, first + number)}
    along_z(NEAR, lambda s: rg.at[0, 0], lambda t: rg.at[0, t], (rzs, 0), lambda t: (rzr, group_of[t]))
    loads[1].wait()
    send(actv.at[mine], actv.at[theirs], (exs, 0), (exr, 0), other)
    for cp in loads[2:]:
        cp.wait()
    cen[mine, :] = (actv[mine, :].astype(F32) - meanv[...]).astype(BF16)
    slot_iota = lax.broadcasted_iota(I32, (1, TOK), 1)
    lab[0, 0, 0] = jnp.where(slot_iota < cntv[...], labv[...], -1)

    for g, (first, number) in enumerate(GROUPS):
        fresh = max(first, 1)
        got(rg.at[0, fresh : first + number], (rzr, g))
        zs = pl.ds(first, number)
        along_x(lambda s: rg.at[0, zs], lambda t: rg.at[t, zs], (rxs, 0), lambda t: (rxr, t))

    along_z(NEAR, lambda s: lab.at[0, 0, 0], lambda t: lab.at[0, 0, t], (bzs, 0), lambda t: (bzr, 0))
    along_z(NEAR, lambda s: lg.at[0, 0], lambda t: lg.at[0, t], (lzs, 0), lambda t: (lzr, 0))
    got(actv.at[theirs], (exr, 0))
    cen[theirs, :] = (actv[theirs, :].astype(F32) - meanv[...]).astype(BF16)

    def block(s, turn=0):
        return pl.ds(pl.multiple_of(lax.rem(y + ZORD[s] + turn, NY) * YB, YB), YB)

    def chunk(k):
        for xs in (2 * k, 2 * k + 1):
            if xs:
                got(rg.at[xs], (rxr, xs))
        rmat = rg[2 * k : 2 * k + 2].astype(F32).reshape(K2, D).astype(BF16)
        part = lax.dot_general(cen[...], rmat, (((1,), (1,)), ((), ())), preferred_element_type=F32)
        pbuf[k] = part.astype(BF16)
        along_y(FAR, lambda s: pbuf.at[k, block(s)], lambda t: prx.at[k, t], (pss, k), lambda t: (psr, k))

    def across(k, s):
        ref, there = cbuf.at[0, k, block(s)], cbuf.at[1, k, block(s, NY // 2)]
        send(ref, there, (fcs, k), (fcr, k), other)

    def reduce(k):
        total = pbuf[k, block(0), :].astype(F32)
        got(prx.at[k, 1:NY], (psr, k))
        for s in range(1, NY):
            total = total + prx[k, s].astype(F32)
        own = cbuf.at[0, k, block(0)]
        own[...] = total.astype(BF16)
        along_y(FAR, lambda s: own, lambda t: own, (css, k), lambda t: (csr, k * NY + t))
        across(k, 0)

    def gathered(k):
        for s in range(1, NY):
            got(cbuf.at[0, k, block(s)], (csr, k * NY + s))
            across(k, s)

    chunk(0)
    chunk(1)
    got(lab.at[0, 0, 1:NZ], (bzr, 0))
    along_x(lambda s: lab.at[0, 0], lambda t: lab.at[0, t], (bxs, 0), lambda t: (bxr, 0))
    got(lg.at[0, 1:NZ], (lzr, 0))
    along_x(lambda s: lg.at[0], lambda t: lg.at[t], (lxs, 0), lambda t: (lxr, 0))

    reduce(0)
    reduce(1)

    got(lab.at[0, 1:NX], (bxr, 0))
    send(lab.at[0], lab.at[1], (exs, 1), (exr, 1), other)
    got(lg.at[1:NX], (lxr, 0))
    half, their_half = pl.ds(pl.multiple_of(c * H, H), H), pl.ds(pl.multiple_of(oc * H, H), H)
    send(lg.at[:, :, :, their_half], lo, (exs, 2), (exr, 2), other)
    lm[0:256, :] = lg[:, :, :, half].astype(F32).reshape(256, H).astype(BF16)
    got(lab.at[1], (exr, 1))
    chip = z * NX + x
    own_class = chip * (2 * RD) + lax.broadcasted_iota(I32, (2 * RD, TOK), 0)
    hits, valid = jnp.zeros((2 * RD, TOK), F32), jnp.zeros((1, TOK), F32)
    for k in range(2):
        for xs in range(NX):
            for zs in range(NZ):
                row = lab[k, xs, zs]
                hits = hits + (row == own_class).astype(F32)
                valid = valid + (row >= 0).astype(F32)
    own_counts = jnp.sum(hits, axis=1, keepdims=True)
    grand = jnp.sum(valid, axis=1, keepdims=True)
    tokens = jnp.concatenate([lab[0, 0, 0], lab[1, 0, 0]], axis=1)
    for xs in range(NX):
        for zs in range(NZ):
            r = lax.broadcasted_iota(I32, (2 * RD, T2), 0)
            owner = lax.rem(z + ZORD[zs], NZ) * NX + lax.rem(x + XORD[xs], NX)
            at = (xs * NZ + zs) * 2 * RD
            oh[at : at + 2 * RD, :] = (owner * (2 * RD) + r == tokens).astype(F32).astype(BF16)

    gathered(0)
    got(lo, (exr, 2))
    lm[256:512, :] = lo[...].astype(F32).reshape(256, H).astype(BF16)
    gathered(1)
    for k in range(2):
        got(cbuf.at[1, k], (fcr, k))

    coords = jnp.concatenate([cbuf[0, 0], cbuf[0, 1], cbuf[1, 0], cbuf[1, 1]], axis=1)
    for q in range(QN):
        cols = slice(q * QW, (q + 1) * QW)
        corr = jnp.dot(coords, lm[:, cols], preferred_element_type=F32)
        acols = pl.ds(pl.multiple_of(c * H + q * QW, QW), QW)
        er[:, cols] = (actv[:, acols].astype(F32) - corr).astype(BF16)
        sums = jnp.dot(oh[...], er[:, cols], preferred_element_type=F32)
        s0[:, cols] = sums[:128]
        txs[:, cols] = jnp.sum(sums, axis=0, keepdims=True)
        for s in range(1, NX):
            sxs[q, s] = sums[s * 128 : (s + 1) * 128].astype(BF16)
        along_x(lambda s: sxs.at[q, s], lambda t: sxr.at[q, t], (xxs, q), lambda t: (xxr, q))
    along_x(lambda s: txs, lambda t: txr.at[t], (xxs, QN), lambda t: (xxr, QN))
    keep = pltpu.make_async_copy(er.at[mine], out.at[:, half], loc.at[6])
    keep.start()
    send(er.at[theirs], out.at[:, half], (exs, 3), (exr, 3), other)

    for q in range(QN):
        cols = slice(q * QW, (q + 1) * QW)
        total = s0[:, cols]
        got(sxr.at[q, 1:NX], (xxr, q))
        for s in range(1, NX):
            total = total + sxr[q, s].astype(F32)
        for s in NEAR:
            szs[q, s] = total[s * 2 * RD : (s + 1) * 2 * RD, :].astype(BF16)
        s0[0 : 2 * RD, cols] = total[0 : 2 * RD]
        along_z(FAR, lambda s: szs.at[q, s], lambda t: szr.at[q, t], (zzs, q), lambda t: (zzr, q))
    total = txs[...]
    got(txr.at[1:NX], (xxr, QN))
    for s in range(1, NX):
        total = total + txr[s]
    tzs[...] = total
    along_z(FAR, lambda s: tzs, lambda t: tzr.at[t], (zzs, QN), lambda t: (zzr, QN))

    scale = 1.0 / jnp.sqrt(jnp.maximum(own_counts, 1.0))
    got(szr.at[0, 1:NZ], (zzr, 0))
    got(szr.at[1, 1:NZ], (zzr, 1))
    got(tzr.at[1:NZ], (zzr, QN))
    for s in range(1, NZ):
        total = total + tzr[s]
    feature_mean = total / grand
    for q in range(QN):
        cols = slice(q * QW, (q + 1) * QW)
        class_sums = s0[0 : 2 * RD, cols]
        for s in range(1, NZ):
            class_sums = class_sums + szr[q, s].astype(F32)
        fin[:, cols] = (class_sums - own_counts * feature_mean[:, cols]) * scale
    own_fin = fin.at[pl.ds(pl.multiple_of(c * RD, RD), RD)]
    send(fin.at[pl.ds(pl.multiple_of(oc * RD, RD), RD)], scores.at[:, half], (exs, 4), (exr, 4), other)
    put = pltpu.make_async_copy(own_fin, scores.at[:, half], loc.at[7])
    put.start()
    lane = lax.broadcasted_iota(I32, (2 * RD, RD), 1)
    row = lax.broadcasted_iota(I32, (2 * RD, RD), 0)
    cnt[...] = jnp.sum(jnp.where(lane + c * RD == row, own_counts, 0.0), axis=0, keepdims=True).astype(I32)

    keep.wait()
    gone(rg.at[0, 1:NZ], (rzs, 0))
    gone(rg.at[1:NX], (rxs, 0))
    gone(lab.at[0, 0, 1:NZ], (bzs, 0))
    gone(lg.at[0, 1:NZ], (lzs, 0))
    gone(lab.at[0, 1:NX], (bxs, 0))
    gone(lg.at[1:NX], (lxs, 0))
    gone(actv.at[mine], (exs, 0))
    gone(lab.at[0], (exs, 1))
    gone(lo, (exs, 2))
    gone(er.at[theirs], (exs, 3))
    for k in range(2):
        gone(prx.at[k, 1:NY], (pss, k))
        gone(prx.at[k, 1:NY], (css, k))
        gone(cbuf.at[0, k], (fcs, k))
    for q in range(QN):
        gone(sxr.at[q, 1:NX], (xxs, q))
        gone(szr.at[q, 1:NZ], (zzs, q))
    gone(txr.at[1:NX], (xxs, QN))
    gone(tzr.at[1:NZ], (zzs, QN))
    gone(own_fin, (exs, 4))
    got(er.at[theirs], (exr, 3))
    put.wait()
    got(own_fin, (exr, 4))


def hand_out(erased, scores, cnt, erased_out, scores_out, cnt_out, sems):
    pairs = ((erased, erased_out), (scores, scores_out), (cnt, cnt_out))
    copies = [pltpu.make_async_copy(a, b, sems.at[i]) for i, (a, b) in enumerate(pairs)]
    for cp in copies:
        cp.start()
    for cp in copies:
        cp.wait()


def per_device(acts, mean_vec, left_factor, right_factor, labels, counts):
    dma = pltpu.SemaphoreType.DMA
    ng = len(GROUPS)
    vm, anywhere = pl.BlockSpec(memory_space=pltpu.VMEM), pl.BlockSpec(memory_space=pl.ANY)
    hbm = pl.BlockSpec(memory_space=pltpu.HBM)
    shapes = (
        jax.ShapeDtypeStruct((TOK, D), BF16),
        jax.ShapeDtypeStruct((RD, D), F32),
        jax.ShapeDtypeStruct((1, RD), I32),
    )
    results = pl.pallas_call(
        kernel,
        out_shape=shapes,
        in_specs=[hbm] * 6,
        out_specs=(anywhere, anywhere, vm),
        scratch_shapes=[
            pltpu.VMEM((1, D), F32),
            pltpu.VMEM((1, TOK), I32),
            pltpu.VMEM((1, 1), I32),
            pltpu.VMEM((T2, D), BF16),
            pltpu.VMEM((T2, D), BF16),
            pltpu.VMEM((NX, NZ, RD, D), BF16),
            pltpu.VMEM((NX, NZ, RD, D), BF16),
            pltpu.VMEM((NX, NZ, RD, H), BF16),
            pltpu.VMEM((C, H), BF16),
            pltpu.VMEM((2, NX, NZ, 1, TOK), I32),
            pltpu.VMEM((2, T2, K2), BF16),
            pltpu.VMEM((2, NY, YB, K2), BF16),
            pltpu.VMEM((2, 2, T2, K2), BF16),
            pltpu.VMEM((C, T2), BF16),
            pltpu.VMEM((T2, H), BF16),
            pltpu.VMEM((QN, NX, 128, QW), BF16),
            pltpu.VMEM((QN, NX, 128, QW), BF16),
            pltpu.VMEM((128, H), F32),
            pltpu.VMEM((1, H), F32),
            pltpu.VMEM((NX, 1, H), F32),
            pltpu.VMEM((QN, NZ, 2 * RD, QW), BF16),
            pltpu.VMEM((QN, NZ, 2 * RD, QW), BF16),
            pltpu.VMEM((1, H), F32),
            pltpu.VMEM((NZ, 1, H), F32),
            pltpu.VMEM((2 * RD, H), F32),
            dma((8,)),
            dma((1,)), dma((ng,)),
            dma((1,)), dma((NX,)),
            dma((1,)), dma((1,)),
            dma((1,)), dma((1,)),
            dma((1,)), dma((1,)),
            dma((1,)), dma((1,)),
            dma((5,)), dma((5,)),
            dma((2,)), dma((2,)),
            dma((2,)), dma((2 * NY,)),
            dma((2,)), dma((2,)),
            dma((QN + 1,)), dma((QN + 1,)),
            dma((QN + 1,)), dma((QN + 1,)),
        ],
        compiler_params=pltpu.CompilerParams(
            collective_id=0, has_side_effects=True, vmem_limit_bytes=VLIM
        ),
        cost_estimate=pl.CostEstimate(flops=6 * 256 * 1024 * 512, bytes_accessed=4 << 20, transcendentals=0),
    )(
        acts,
        mean_vec.reshape(1, D),
        left_factor,
        right_factor,
        labels.reshape(1, TOK),
        counts.reshape(1, 1),
    )
    erased, scores, cnt = pl.pallas_call(
        hand_out,
        out_shape=shapes,
        in_specs=[vm] * 3,
        out_specs=(hbm,) * 3,
        scratch_shapes=[dma((3,))],
    )(*results)
    return erased, scores, cnt.reshape(RD)


def solution(mesh):
    return jax.shard_map(
        per_device,
        mesh=mesh,
        in_specs=(
            P("dp", "tensor"),
            P("tensor"),
            P("dp", "tensor"),
            P("dp", "tensor"),
            P("dp"),
            P("dp"),
        ),
        out_specs=(P("dp", "tensor"), P("dp", "tensor"), P("dp")),
        check_vma=False,
    )
```

```python
import functools

import jax
import jax.numpy as jnp
from jax import lax
from jax.experimental import pallas as pl
from jax.experimental.pallas import tpu as pltpu
from jax.sharding import PartitionSpec as P

MESH = pl.DeviceIdType.MESH
F32, BF16, I32 = jnp.float32, jnp.bfloat16, jnp.int32
C = 512
NZ, NX, NY = 8, 4, 8
ZORD = (0, 1, 7, 2, 6, 3, 5, 4)
XORD = (0, 1, 3, 2)
ZBACK = tuple(ZORD.index((NZ - d) % NZ) for d in ZORD)
XBACK = tuple(XORD.index((NX - d) % NX) for d in XORD)
NEAR, FAR = (1, 2, 3, 4, 5, 6, 7), (7, 6, 5, 4, 3, 2, 1)
XFIRST = (2, 3, 1)
GROUPS = ((0, 2), (2, 2), (4, 2), (6, 2))
TOK, D, RD = 256, 1024, 8
T2, H, K2 = 512, 512, 128
M = 24
YB = T2 // NY
VLIM = 63 << 20


def kernel(
    acts, mean, left, right, labels, counts,
    out, scores, cnt,
    meanv, labv, cntv, actv, cen, rg, lg, lo, lm, lab, labo, pbuf, prx, cbuf, oh, er,
    sxs, sxr, s0, txs, txr, szs, szr, tzs, tzr, mh, rall, gy, gx, fin,
    loc, rzs, rzr, rxs, rxr, lzs, lzr, lxs, lxr, bzs, bzr, bxs, bxr, exs, exr,
    pss, psr, css, csr, fcs, fcr, xxs, xxr, zzs, zzr, ggs, ggr,
):
    dp, y = lax.axis_index("dp"), lax.axis_index("tensor")
    c, x, z = lax.rem(dp, 2), lax.rem(dp // 2, NX), dp // (2 * NX)
    oc = 1 - c

    def dev(dz=0, dx=0, dy=0, core=None):
        core = c if core is None else core
        zz, xx, yy = lax.rem(z + dz, NZ), lax.rem(x + dx, NX), lax.rem(y + dy, NY)
        return ((zz * NX + xx) * 2 + core, yy)

    other = dev(core=oc)

    def send(src, dst, ss, rs, to):
        pltpu.make_async_remote_copy(
            src_ref=src,
            dst_ref=dst,
            send_sem=ss[0].at[ss[1]],
            recv_sem=rs[0].at[rs[1]],
            device_id=to,
            device_id_type=MESH,
        ).start()

    def got(ref, rs):
        sem = rs[0].at[rs[1]]
        pltpu.make_async_remote_copy(
            src_ref=ref, dst_ref=ref, send_sem=sem, recv_sem=sem, device_id=other, device_id_type=MESH
        ).wait_recv()

    def gone(ref, ss):
        sem = ss[0].at[ss[1]]
        pltpu.make_async_remote_copy(
            src_ref=ref, dst_ref=ref, send_sem=sem, recv_sem=sem, device_id=other, device_id_type=MESH
        ).wait_send()

    def along_z(order, src, dst, ss, rs):
        for s in order:
            send(src(s), dst(ZBACK[s]), ss, rs(ZBACK[s]), dev(dz=ZORD[s]))

    def along_y(order, src, dst, ss, rs):
        for s in order:
            send(src(s), dst(ZBACK[s]), ss, rs(ZBACK[s]), dev(dy=ZORD[s]))

    def along_x(src, dst, ss, rs):
        for s in XFIRST:
            send(src(s), dst(XBACK[s]), ss, rs(XBACK[s]), dev(dx=XORD[s]))

    mine, theirs = pl.ds(0, TOK), pl.ds(TOK, TOK)
    loads = [
        pltpu.make_async_copy(src, dst, loc.at[i])
        for i, (src, dst) in enumerate(
            (
                (right, rg.at[0, 0]),
                (acts, actv.at[mine]),
                (mean, meanv),
                (labels, labv),
                (counts, cntv),
                (left, lg.at[0, 0]),
            )
        )
    ]
    for cp in loads:
        cp.start()

    barrier = pltpu.get_barrier_semaphore()
    peers = [dev(dz=ZORD[s]) for s in FAR] + [dev(dy=ZORD[s]) for s in FAR]
    peers += [dev(dx=d) for d in (2, 1, 3)] + [other]
    for p in peers:
        pl.semaphore_signal(barrier, inc=1, device_id=p, device_id_type=MESH)
    loads[0].wait()
    pl.semaphore_wait(barrier, len(peers))

    group_of = {s: g for g, (first, number) in enumerate(GROUPS) for s in range(first, first + number)}
    along_z(NEAR, lambda s: rg.at[0, 0], lambda t: rg.at[0, t], (rzs, 0), lambda t: (rzr, group_of[t]))
    loads[1].wait()
    send(actv.at[mine], actv.at[theirs], (exs, 0), (exr, 0), other)
    for cp in loads[2:]:
        cp.wait()
    cen[mine, :] = (actv[mine, :].astype(F32) - meanv[...]).astype(BF16)
    slot_iota = lax.broadcasted_iota(I32, (1, TOK), 1)
    lab[0, 0, 0] = jnp.where(slot_iota < cntv[0], labv[...], -1)
    send(lab.at[0, 0, 0], labo, (exs, 5), (exr, 5), other)

    def right_x(g):
        first, number = GROUPS[g]
        got(rg.at[0, max(first, 1) : first + number], (rzr, g))
        zs = pl.ds(first, number)
        along_x(lambda s: rg.at[0, zs], lambda t: rg.at[t, zs], (rxs, 0), lambda t: (rxr, first // 4))

    half, their_half = pl.ds(pl.multiple_of(c * H, H), H), pl.ds(pl.multiple_of(oc * H, H), H)
    right_x(0)
    right_x(1)
    got(labo, (exr, 5))
    tokens = jnp.concatenate([lab[0, 0, 0], labo[...]], axis=1)
    for xs in range(NX):
        for zs in range(NZ):
            r = lax.broadcasted_iota(I32, (2 * RD, T2), 0)
            owner = lax.rem(z + ZORD[zs], NZ) * NX + lax.rem(x + XORD[xs], NX)
            at = (xs * NZ + zs) * 2 * RD
            oh[at : at + 2 * RD, :] = (owner * (2 * RD) + r == tokens).astype(F32).astype(BF16)
    got(actv.at[theirs], (exr, 0))
    cen[theirs, :] = (actv[theirs, :].astype(F32) - meanv[...]).astype(BF16)
    sums = jnp.dot(oh[...], actv[:, half], preferred_element_type=F32)
    s0[...] = sums[:128]
    txs[...] = jnp.sum(sums, axis=0, keepdims=True)
    for s in range(1, NX):
        sxs[s] = sums[s * 128 : (s + 1) * 128].astype(BF16)
    right_x(2)
    right_x(3)
    along_x(lambda s: sxs.at[s], lambda t: sxr.at[t], (xxs, 0), lambda t: (xxr, 0))
    along_x(lambda s: txs, lambda t: txr.at[t], (xxs, 1), lambda t: (xxr, 1))
    along_z(NEAR, lambda s: lab.at[0, 0, 0], lambda t: lab.at[0, 0, t], (bzs, 0), lambda t: (bzr, 0))

    def block(s, turn=0):
        return pl.ds(pl.multiple_of(lax.rem(y + ZORD[s] + turn, NY) * YB, YB), YB)

    def chunk(k):
        got(rg.at[1:NX, 4 * k : 4 * k + 4], (rxr, k))
        rmat = rg[:, 4 * k : 4 * k + 4].astype(F32).reshape(K2, D).astype(BF16)
        rall[k * K2 : (k + 1) * K2, :] = rmat
        part = lax.dot_general(cen[...], rmat, (((1,), (1,)), ((), ())), preferred_element_type=F32)
        pbuf[k] = part.astype(BF16)
        along_y(FAR, lambda s: pbuf.at[k, block(s)], lambda t: prx.at[k, t], (pss, k), lambda t: (psr, k))

    def across(k, s):
        ref, there = cbuf.at[0, k, block(s)], cbuf.at[1, k, block(s, NY // 2)]
        send(ref, there, (fcs, k), (fcr, k), other)

    def reduce(k):
        total = pbuf[k, block(0), :].astype(F32)
        got(prx.at[k, 1:NY], (psr, k))
        for s in range(1, NY):
            total = total + prx[k, s].astype(F32)
        own = cbuf.at[0, k, block(0)]
        own[...] = total.astype(BF16)
        along_y(FAR, lambda s: own, lambda t: own, (css, k), lambda t: (csr, k * NY + t))
        across(k, 0)

    def gathered(k):
        for s in range(1, NY):
            got(cbuf.at[0, k, block(s)], (csr, k * NY + s))
            across(k, s)

    along_z(NEAR, lambda s: lg.at[0, 0], lambda t: lg.at[0, t], (lzs, 0), lambda t: (lzr, 0))
    chunk(0)
    got(lab.at[0, 0, 1:NZ], (bzr, 0))
    along_x(lambda s: lab.at[0, 0], lambda t: lab.at[0, t], (bxs, 0), lambda t: (bxr, 0))
    chunk(1)
    got(lg.at[0, 1:NZ], (lzr, 0))
    along_x(lambda s: lg.at[0], lambda t: lg.at[t], (lxs, 0), lambda t: (lxr, 0))
    got(lab.at[0, 1:NX], (bxr, 0))
    send(lab.at[0], lab.at[1], (exs, 1), (exr, 1), other)

    reduce(0)
    total = s0[...]
    got(sxr.at[1:NX], (xxr, 0))
    for s in range(1, NX):
        total = total + sxr[s].astype(F32)
    for s in NEAR:
        szs[s] = total[s * 2 * RD : (s + 1) * 2 * RD, :].astype(BF16)
    mh[0, 0 : 2 * RD, :] = total[0 : 2 * RD]
    along_z(FAR, lambda s: szs.at[s], lambda t: szr.at[t], (zzs, 0), lambda t: (zzr, 0))
    total = txs[...]
    got(txr.at[1:NX], (xxr, 1))
    for s in range(1, NX):
        total = total + txr[s]
    tzs[...] = total
    along_z(FAR, lambda s: tzs, lambda t: tzr.at[t], (zzs, 1), lambda t: (zzr, 1))
    reduce(1)

    got(lab.at[1], (exr, 1))
    chip = z * NX + x
    own_class = chip * (2 * RD) + lax.broadcasted_iota(I32, (2 * RD, TOK), 0)
    hits, valid = jnp.zeros((2 * RD, TOK), F32), jnp.zeros((1, TOK), F32)
    for k in range(2):
        for xs in range(NX):
            for zs in range(NZ):
                row = lab[k, xs, zs]
                hits = hits + (row == own_class).astype(F32)
                valid = valid + (row >= 0).astype(F32)
    own_counts = jnp.sum(hits, axis=1, keepdims=True)
    grand = jnp.sum(valid, axis=1, keepdims=True)
    every = jnp.concatenate([own_counts, jnp.broadcast_to(grand, (M - 2 * RD, 1))], axis=0)

    gathered(0)
    got(lg.at[1:NX], (lxr, 0))
    send(lg.at[:, :, :, their_half], lo, (exs, 2), (exr, 2), other)
    for k in range(2):
        lm[k * K2 : (k + 1) * K2, :] = lg[:, 4 * k : 4 * k + 4, :, half].astype(F32).reshape(K2, H).astype(BF16)

    got(szr.at[1:NZ], (zzr, 0))
    got(tzr.at[1:NZ], (zzr, 1))
    class_sums, total = mh[0, 0 : 2 * RD, :], tzs[...]
    for s in range(1, NZ):
        class_sums = class_sums + szr[s].astype(F32)
        total = total + tzr[s]
    mh[0, 0 : 2 * RD, :] = class_sums
    mh[0, 2 * RD : M, :] = jnp.broadcast_to(total, (M - 2 * RD, H))
    send(mh.at[0], mh.at[1], (exs, 6), (exr, 6), other)
    gathered(1)

    def twice(a, b, dims):
        high = a.astype(BF16)
        low = (a - high.astype(F32)).astype(BF16)
        dims = (dims, ((), ()))
        return lax.dot_general(high, b, dims, preferred_element_type=F32) + lax.dot_general(
            low, b, dims, preferred_element_type=F32
        )

    got(mh.at[1], (exr, 6))
    gsum = twice(mh[0] - every * meanv[:, half], rall[:, half], ((1,), (1,)))
    gsum = gsum + twice(mh[1] - every * meanv[:, their_half], rall[:, their_half], ((1,), (1,)))
    gy[0] = gsum
    along_y(FAR, lambda s: gy.at[0], lambda t: gy.at[t], (ggs, 0), lambda t: (ggr, 0))

    got(lo, (exr, 2))
    for k in range(2, 4):
        lm[k * K2 : (k + 1) * K2, :] = lo[:, 4 * k - 8 : 4 * k - 4].astype(F32).reshape(K2, H).astype(BF16)
    for k in range(2):
        got(cbuf.at[1, k], (fcr, k))

    coords = jnp.concatenate([cbuf[0, 0], cbuf[0, 1], cbuf[1, 0], cbuf[1, 1]], axis=1)
    for rows in (theirs, mine):
        at = rows.start
        corr = jnp.dot(coords[at : at + TOK], lm[...], preferred_element_type=F32)
        er[rows, :] = (actv[rows, half].astype(F32) - corr).astype(BF16)
        if at:
            send(er.at[theirs], out.at[:, half], (exs, 3), (exr, 3), other)
    keep = pltpu.make_async_copy(er.at[mine], out.at[:, half], loc.at[6])
    keep.start()

    got(gy.at[1:NY], (ggr, 0))
    for s in range(1, NY):
        gsum = gsum + gy[s]
    gx[0] = gsum
    send(gx.at[0], gx.at[1], (exs, 7), (exr, 7), other)
    result = mh[0] - twice(gsum, lm[0:256, :], ((1,), (0,)))
    got(gx.at[1], (exr, 7))
    result = result - twice(gx[1], lm[256:512, :], ((1,), (0,)))
    scale = 1.0 / jnp.sqrt(jnp.maximum(own_counts, 1.0))
    feature_mean = result[2 * RD : 2 * RD + 1, :] / grand
    fin[...] = (result[0 : 2 * RD] - own_counts * feature_mean) * scale
    own_fin = fin.at[pl.ds(pl.multiple_of(c * RD, RD), RD)]
    send(fin.at[pl.ds(pl.multiple_of(oc * RD, RD), RD)], scores.at[:, half], (exs, 4), (exr, 4), other)
    put = pltpu.make_async_copy(own_fin, scores.at[:, half], loc.at[7])
    put.start()
    lane = lax.broadcasted_iota(I32, (2 * RD, RD), 1)
    row = lax.broadcasted_iota(I32, (2 * RD, RD), 0)
    cnt[...] = jnp.sum(jnp.where(lane + c * RD == row, own_counts, 0.0), axis=0, keepdims=True).astype(I32)

    keep.wait()
    gone(rg.at[0, 1:NZ], (rzs, 0))
    gone(rg.at[1:NX], (rxs, 0))
    gone(lab.at[0, 0, 1:NZ], (bzs, 0))
    gone(lg.at[0, 1:NZ], (lzs, 0))
    gone(lab.at[0, 1:NX], (bxs, 0))
    gone(lg.at[1:NX], (lxs, 0))
    gone(actv.at[mine], (exs, 0))
    gone(lab.at[0], (exs, 1))
    gone(lo, (exs, 2))
    gone(er.at[theirs], (exs, 3))
    for k in range(2):
        gone(prx.at[k, 1:NY], (pss, k))
        gone(prx.at[k, 1:NY], (css, k))
        gone(cbuf.at[0, k], (fcs, k))
    gone(sxr.at[1:NX], (xxs, 0))
    gone(szr.at[1:NZ], (zzs, 0))
    gone(txr.at[1:NX], (xxs, 1))
    gone(tzr.at[1:NZ], (zzs, 1))
    gone(gy.at[1:NY], (ggs, 0))
    gone(labo, (exs, 5))
    gone(mh.at[0], (exs, 6))
    gone(gx.at[0], (exs, 7))
    gone(own_fin, (exs, 4))
    got(er.at[theirs], (exr, 3))
    put.wait()
    got(own_fin, (exr, 4))


def hand_out(erased, scores, cnt, erased_out, scores_out, cnt_out, sems):
    pairs = ((erased, erased_out), (scores, scores_out), (cnt, cnt_out))
    copies = [pltpu.make_async_copy(a, b, sems.at[i]) for i, (a, b) in enumerate(pairs)]
    for cp in copies:
        cp.start()
    for cp in copies:
        cp.wait()


def per_device(acts, mean_vec, left_factor, right_factor, labels, counts):
    dma = pltpu.SemaphoreType.DMA
    ng = len(GROUPS)
    vm, anywhere = pl.BlockSpec(memory_space=pltpu.VMEM), pl.BlockSpec(memory_space=pl.ANY)
    hbm = pl.BlockSpec(memory_space=pltpu.HBM)
    shapes = (
        jax.ShapeDtypeStruct((TOK, D), BF16),
        jax.ShapeDtypeStruct((RD, D), F32),
        jax.ShapeDtypeStruct((1, RD), I32),
    )
    results = pl.pallas_call(
        kernel,
        out_shape=shapes,
        in_specs=[hbm] * 6,
        out_specs=(anywhere, anywhere, vm),
        scratch_shapes=[
            pltpu.VMEM((1, D), F32),
            pltpu.VMEM((1, TOK), I32),
            pltpu.SMEM((1,), I32),
            pltpu.VMEM((T2, D), BF16),
            pltpu.VMEM((T2, D), BF16),
            pltpu.VMEM((NX, NZ, RD, D), BF16),
            pltpu.VMEM((NX, NZ, RD, D), BF16),
            pltpu.VMEM((NX, NZ, RD, H), BF16),
            pltpu.VMEM((C, H), BF16),
            pltpu.VMEM((2, NX, NZ, 1, TOK), I32),
            pltpu.VMEM((1, TOK), I32),
            pltpu.VMEM((2, T2, K2), BF16),
            pltpu.VMEM((2, NY, YB, K2), BF16),
            pltpu.VMEM((2, 2, T2, K2), BF16),
            pltpu.VMEM((C, T2), BF16),
            pltpu.VMEM((T2, H), BF16),
            pltpu.VMEM((NX, 128, H), BF16),
            pltpu.VMEM((NX, 128, H), BF16),
            pltpu.VMEM((128, H), F32),
            pltpu.VMEM((1, H), F32),
            pltpu.VMEM((NX, 1, H), F32),
            pltpu.VMEM((NZ, 2 * RD, H), BF16),
            pltpu.VMEM((NZ, 2 * RD, H), BF16),
            pltpu.VMEM((1, H), F32),
            pltpu.VMEM((NZ, 1, H), F32),
            pltpu.VMEM((2, M, H), F32),
            pltpu.VMEM((256, D), BF16),
            pltpu.VMEM((NY, M, 256), F32),
            pltpu.VMEM((2, M, 256), F32),
            pltpu.VMEM((2 * RD, H), F32),
            dma((8,)),
            dma((1,)), dma((ng,)),
            dma((1,)), dma((2,)),
            dma((1,)), dma((1,)),
            dma((1,)), dma((1,)),
            dma((1,)), dma((1,)),
            dma((1,)), dma((1,)),
            dma((8,)), dma((8,)),
            dma((2,)), dma((2,)),
            dma((2,)), dma((2 * NY,)),
            dma((2,)), dma((2,)),
            dma((2,)), dma((2,)),
            dma((2,)), dma((2,)),
            dma((1,)), dma((1,)),
        ],
        compiler_params=pltpu.CompilerParams(
            collective_id=0, has_side_effects=True, vmem_limit_bytes=VLIM
        ),
        cost_estimate=pl.CostEstimate(flops=6 * 256 * 1024 * 512, bytes_accessed=4 << 20, transcendentals=0),
    )(
        acts,
        mean_vec.reshape(1, D),
        left_factor,
        right_factor,
        labels.reshape(1, TOK),
        counts,
    )
    erased, scores, cnt = pl.pallas_call(
        hand_out,
        out_shape=shapes,
        in_specs=[vm] * 3,
        out_specs=(hbm,) * 3,
        scratch_shapes=[dma((3,))],
    )(*results)
    return erased, scores, cnt.reshape(RD)


def solution(mesh):
    return jax.shard_map(
        per_device,
        mesh=mesh,
        in_specs=(
            P("dp", "tensor"),
            P("tensor"),
            P("dp", "tensor"),
            P("dp", "tensor"),
            P("dp"),
            P("dp"),
        ),
        out_specs=(P("dp", "tensor"), P("dp", "tensor"), P("dp")),
        check_vma=False,
    )
```

```python
import functools

import jax
import jax.numpy as jnp
from jax import lax
from jax.experimental import pallas as pl
from jax.experimental.pallas import tpu as pltpu
from jax.sharding import PartitionSpec as P

MESH = pl.DeviceIdType.MESH
F32, BF16, I32 = jnp.float32, jnp.bfloat16, jnp.int32
C = 512
NZ, NX, NY = 8, 4, 8
ZORD = (0, 1, 7, 2, 6, 3, 5, 4)
XORD = (0, 1, 3, 2)
ZBACK = tuple(ZORD.index((NZ - d) % NZ) for d in ZORD)
XBACK = tuple(XORD.index((NX - d) % NX) for d in XORD)
NEAR, FAR = (1, 2, 3, 4, 5, 6, 7), (7, 6, 5, 4, 3, 2, 1)
XFIRST = (2, 3, 1)
GROUPS = ((0, 2), (2, 2), (4, 2), (6, 2))
TOK, D, RD = 256, 1024, 8
T2, H, K2 = 512, 512, 128
M = 2 * RD
YB = T2 // NY
VLIM = 63 << 20
PIECES = 4


def kernel(
    acts, mean, left, right, labels, counts,
    out, scores, cnt,
    meanv, labv, cntv, actv, cen, rg, lg, lo, lm, lab, labo, pbuf, prx, cbuf, oh, er,
    sxs, sxr, s0, txs, txr, szs, szr, tzs, tzr, mh, rall, gy, gx, cnts,
    loc, rzs, rzr, rxs, rxr, lzs, lzr, lxs, lxr, bzs, bzr, bxs, bxr, exs, exr,
    pss, psr, css, csr, fcs, fcr, xxs, xxr, zzs, zzr, ggs, ggr,
):
    dp, y = lax.axis_index("dp"), lax.axis_index("tensor")
    c, x, z = lax.rem(dp, 2), lax.rem(dp // 2, NX), dp // (2 * NX)
    oc = 1 - c

    def dev(dz=0, dx=0, dy=0, core=None):
        core = c if core is None else core
        zz, xx, yy = lax.rem(z + dz, NZ), lax.rem(x + dx, NX), lax.rem(y + dy, NY)
        return ((zz * NX + xx) * 2 + core, yy)

    other = dev(core=oc)

    def send(src, dst, ss, rs, to):
        pltpu.make_async_remote_copy(
            src_ref=src,
            dst_ref=dst,
            send_sem=ss[0].at[ss[1]],
            recv_sem=rs[0].at[rs[1]],
            device_id=to,
            device_id_type=MESH,
        ).start()

    def got(ref, rs):
        sem = rs[0].at[rs[1]]
        pltpu.make_async_remote_copy(
            src_ref=ref, dst_ref=ref, send_sem=sem, recv_sem=sem, device_id=other, device_id_type=MESH
        ).wait_recv()

    def gone(ref, ss):
        sem = ss[0].at[ss[1]]
        pltpu.make_async_remote_copy(
            src_ref=ref, dst_ref=ref, send_sem=sem, recv_sem=sem, device_id=other, device_id_type=MESH
        ).wait_send()

    def along_z(order, src, dst, ss, rs):
        for s in order:
            send(src(s), dst(ZBACK[s]), ss, rs(ZBACK[s]), dev(dz=ZORD[s]))

    def along_y(order, src, dst, ss, rs):
        for s in order:
            send(src(s), dst(ZBACK[s]), ss, rs(ZBACK[s]), dev(dy=ZORD[s]))

    def along_x(src, dst, ss, rs):
        for s in XFIRST:
            send(src(s), dst(XBACK[s]), ss, rs(XBACK[s]), dev(dx=XORD[s]))

    mine, theirs = pl.ds(0, TOK), pl.ds(TOK, TOK)
    loads = [
        pltpu.make_async_copy(src, dst, loc.at[i])
        for i, (src, dst) in enumerate(
            (
                (right, rg.at[0, 0]),
                (acts, actv.at[mine]),
                (mean, meanv),
                (labels, labv),
                (counts, cntv),
                (left, lg.at[0, 0]),
            )
        )
    ]
    for cp in loads:
        cp.start()

    barrier = pltpu.get_barrier_semaphore()
    peers = [dev(dz=ZORD[s]) for s in FAR] + [dev(dy=ZORD[s]) for s in FAR]
    peers += [dev(dx=d) for d in (2, 1, 3)] + [other]
    for p in peers:
        pl.semaphore_signal(barrier, inc=1, device_id=p, device_id_type=MESH)
    loads[0].wait()
    pl.semaphore_wait(barrier, len(peers))

    group_of = {s: g for g, (first, number) in enumerate(GROUPS) for s in range(first, first + number)}
    along_z(NEAR, lambda s: rg.at[0, 0], lambda t: rg.at[0, t], (rzs, 0), lambda t: (rzr, group_of[t]))
    loads[1].wait()
    send(actv.at[mine], actv.at[theirs], (exs, 0), (exr, 0), other)
    for cp in loads[2:]:
        cp.wait()
    cen[mine, :] = (actv[mine, :].astype(F32) - meanv[...]).astype(BF16)
    slot_iota = lax.broadcasted_iota(I32, (1, TOK), 1)
    lab[0, 0, 0] = jnp.where(slot_iota < cntv[0], labv[...], -1)
    send(lab.at[0, 0, 0], labo, (exs, 5), (exr, 5), other)

    def right_x(g):
        first, number = GROUPS[g]
        got(rg.at[0, max(first, 1) : first + number], (rzr, g))
        zs = pl.ds(first, number)
        along_x(lambda s: rg.at[0, zs], lambda t: rg.at[t, zs], (rxs, 0), lambda t: (rxr, first // 4))

    half, their_half = pl.ds(pl.multiple_of(c * H, H), H), pl.ds(pl.multiple_of(oc * H, H), H)
    right_x(0)
    right_x(1)
    got(labo, (exr, 5))
    tokens = jnp.concatenate([lab[0, 0, 0], labo[...]], axis=1)
    for xs in range(NX):
        for zs in range(NZ):
            r = lax.broadcasted_iota(I32, (2 * RD, T2), 0)
            owner = lax.rem(z + ZORD[zs], NZ) * NX + lax.rem(x + XORD[xs], NX)
            at = (xs * NZ + zs) * 2 * RD
            oh[at : at + 2 * RD, :] = (owner * (2 * RD) + r == tokens).astype(F32).astype(BF16)
    got(actv.at[theirs], (exr, 0))
    cen[theirs, :] = (actv[theirs, :].astype(F32) - meanv[...]).astype(BF16)
    sums = jnp.dot(oh[...], actv[:, half], preferred_element_type=F32)
    s0[...] = sums[:128]
    txs[...] = jnp.sum(sums, axis=0, keepdims=True)
    for s in range(1, NX):
        sxs[s] = sums[s * 128 : (s + 1) * 128].astype(BF16)
    right_x(2)
    along_x(lambda s: sxs.at[s], lambda t: sxr.at[t], (xxs, 0), lambda t: (xxr, 0))
    along_x(lambda s: txs, lambda t: txr.at[t], (xxs, 1), lambda t: (xxr, 1))
    right_x(3)
    along_z(NEAR, lambda s: lab.at[0, 0, 0], lambda t: lab.at[0, 0, t], (bzs, 0), lambda t: (bzr, 0))

    def block(s, turn=0):
        return pl.ds(pl.multiple_of(lax.rem(y + ZORD[s] + turn, NY) * YB, YB), YB)

    def chunk(k):
        got(rg.at[1:NX, 4 * k : 4 * k + 4], (rxr, k))
        rmat = rg[:, 4 * k : 4 * k + 4].astype(F32).reshape(K2, D).astype(BF16)
        rall[k * K2 : (k + 1) * K2, :] = rmat
        part = lax.dot_general(cen[...], rmat, (((1,), (1,)), ((), ())), preferred_element_type=F32)
        pbuf[k] = part.astype(BF16)
        along_y(FAR, lambda s: pbuf.at[k, block(s)], lambda t: prx.at[k, t], (pss, k), lambda t: (psr, k))

    def across(k, s):
        ref, there = cbuf.at[0, k, block(s)], cbuf.at[1, k, block(s, NY // 2)]
        send(ref, there, (fcs, k), (fcr, k), other)

    def reduce(k):
        total = pbuf[k, block(0), :].astype(F32)
        got(prx.at[k, 1:NY], (psr, k))
        for s in range(1, NY):
            total = total + prx[k, s].astype(F32)
        own = cbuf.at[0, k, block(0)]
        own[...] = total.astype(BF16)
        along_y(FAR, lambda s: own, lambda t: own, (css, k), lambda t: (csr, k * NY + t))
        across(k, 0)

    def gathered(k):
        for s in range(1, NY):
            got(cbuf.at[0, k, block(s)], (csr, k * NY + s))
            across(k, s)

    along_z(NEAR, lambda s: lg.at[0, 0], lambda t: lg.at[0, t], (lzs, 0), lambda t: (lzr, 0))
    chunk(0)
    got(lab.at[0, 0, 1:NZ], (bzr, 0))
    along_x(lambda s: lab.at[0, 0], lambda t: lab.at[0, t], (bxs, 0), lambda t: (bxr, 0))
    chunk(1)
    got(lg.at[0, 1:NZ], (lzr, 0))
    along_x(lambda s: lg.at[0], lambda t: lg.at[t], (lxs, 0), lambda t: (lxr, 0))
    got(lab.at[0, 1:NX], (bxr, 0))
    send(lab.at[0], lab.at[1], (exs, 1), (exr, 1), other)

    total = s0[...]
    got(sxr.at[1:NX], (xxr, 0))
    for s in range(1, NX):
        total = total + sxr[s].astype(F32)
    for s in NEAR:
        szs[s] = total[s * 2 * RD : (s + 1) * 2 * RD, :].astype(BF16)
    mh[0, 0 : 2 * RD, :] = total[0 : 2 * RD]
    along_z(FAR, lambda s: szs.at[s], lambda t: szr.at[t], (zzs, 0), lambda t: (zzr, 0))
    total = txs[...]
    got(txr.at[1:NX], (xxr, 1))
    for s in range(1, NX):
        total = total + txr[s]
    tzs[...] = total
    along_z(FAR, lambda s: tzs, lambda t: tzr.at[t], (zzs, 1), lambda t: (zzr, 1))
    reduce(0)
    reduce(1)

    got(lab.at[1], (exr, 1))
    chip = z * NX + x
    own_class = chip * (2 * RD) + lax.broadcasted_iota(I32, (2 * RD, TOK), 0)
    hits, valid = jnp.zeros((2 * RD, TOK), F32), jnp.zeros((1, TOK), F32)
    for k in range(2):
        for xs in range(NX):
            for zs in range(NZ):
                row = lab[k, xs, zs]
                hits = hits + (row == own_class).astype(F32)
                valid = valid + (row >= 0).astype(F32)
    own_counts = jnp.sum(hits, axis=1, keepdims=True)
    grand = jnp.sum(valid, axis=1, keepdims=True)

    got(szr.at[1:NZ], (zzr, 0))
    got(tzr.at[1:NZ], (zzr, 1))
    class_sums, total = mh[0], tzs[...]
    for s in range(1, NZ):
        class_sums = class_sums + szr[s].astype(F32)
        total = total + tzr[s]
    mh[0] = class_sums - own_counts * (total / grand)
    send(mh.at[0], mh.at[1], (exs, 6), (exr, 6), other)
    gathered(0)

    def twice(a, b, dims):
        high = a.astype(BF16).astype(F32)
        terms = jnp.concatenate([high, a - high], axis=0).astype(BF16)
        both = lax.dot_general(terms, b, (dims, ((), ())), preferred_element_type=F32)
        return both[: a.shape[0]] + both[a.shape[0] :]

    got(mh.at[1], (exr, 6))
    gsum = twice(mh[0], rall[:, half], ((1,), (1,))) + twice(mh[1], rall[:, their_half], ((1,), (1,)))
    gy[0] = gsum.astype(BF16)
    along_y(FAR, lambda s: gy.at[0], lambda t: gy.at[t], (ggs, 0), lambda t: (ggr, 0))

    got(lg.at[1:NX], (lxr, 0))
    send(lg, lo, (exs, 2), (exr, 2), other)
    for k in range(2):
        lm[k * K2 : (k + 1) * K2, :] = lg[:, 4 * k : 4 * k + 4].astype(F32).reshape(K2, D).astype(BF16)
    gathered(1)
    got(lo, (exr, 2))
    for k in range(2, 4):
        lm[k * K2 : (k + 1) * K2, :] = lo[:, 4 * k - 8 : 4 * k - 4].astype(F32).reshape(K2, D).astype(BF16)
    for k in range(2):
        got(cbuf.at[1, k], (fcr, k))

    coords = jnp.concatenate([cbuf[0, 0], cbuf[0, 1], cbuf[1, 0], cbuf[1, 1]], axis=1)
    for rows in (theirs, mine):
        at = rows.start
        corr = jnp.dot(coords[at : at + TOK], lm[:, half], preferred_element_type=F32)
        er[rows, :] = (actv[rows, half].astype(F32) - corr).astype(BF16)
        if at:
            send(er.at[theirs], out.at[:, half], (exs, 3), (exr, 3), other)
    keep = pltpu.make_async_copy(er.at[mine], out.at[:, half], loc.at[6])
    keep.start()

    got(gy.at[1:NY], (ggr, 0))
    for s in range(1, NY):
        gsum = gsum + gy[s].astype(F32)
    gx[0] = gsum
    ours, others = pl.ds(pl.multiple_of(c * RD, RD), RD), pl.ds(pl.multiple_of(oc * RD, RD), RD)
    send(gx.at[0, others], gx.at[1, others], (exs, 7), (exr, 7), other)
    cnts[...] = jnp.broadcast_to(own_counts, (M, 128))
    own_counts = cnts[ours, 0:1]
    lane = lax.broadcasted_iota(I32, (RD, RD), 1)
    row = lax.broadcasted_iota(I32, (RD, RD), 0)
    cnt[...] = jnp.sum(jnp.where(lane == row, own_counts, 0.0), axis=0, keepdims=True).astype(I32)
    scale = 1.0 / jnp.sqrt(jnp.maximum(own_counts, 1.0))
    got(gx.at[1, ours], (exr, 7))
    coords = jnp.concatenate([gx[0, ours, :], gx[1, ours, :]], axis=1)
    moved = twice(coords, lm[...], ((1,), (0,)))
    scores[...] = moved * -scale
    for k, cols in enumerate((half, their_half)):
        scores[:, cols] += mh[k, ours, :] * scale

    keep.wait()
    gone(rg.at[0, 1:NZ], (rzs, 0))
    gone(rg.at[1:NX], (rxs, 0))
    gone(lab.at[0, 0, 1:NZ], (bzs, 0))
    gone(lg.at[0, 1:NZ], (lzs, 0))
    gone(lab.at[0, 1:NX], (bxs, 0))
    gone(lg.at[1:NX], (lxs, 0))
    gone(actv.at[mine], (exs, 0))
    gone(lab.at[0], (exs, 1))
    gone(lo, (exs, 2))
    gone(er.at[theirs], (exs, 3))
    for k in range(2):
        gone(prx.at[k, 1:NY], (pss, k))
        gone(prx.at[k, 1:NY], (css, k))
        gone(cbuf.at[0, k], (fcs, k))
    gone(sxr.at[1:NX], (xxs, 0))
    gone(szr.at[1:NZ], (zzs, 0))
    gone(txr.at[1:NX], (xxs, 1))
    gone(tzr.at[1:NZ], (zzs, 1))
    gone(gy.at[1:NY], (ggs, 0))
    gone(labo, (exs, 5))
    gone(mh.at[0], (exs, 6))
    gone(gx.at[0, others], (exs, 7))
    got(er.at[theirs], (exr, 3))


def hand_out(erased, scores, cnt, erased_out, scores_out, cnt_out, erased_v, scores_v, cnt_v, sems):
    rows = TOK // PIECES
    parts = [pl.ds(i * rows, rows) for i in range(PIECES)]
    trips = [(erased.at[p], erased_v.at[p], erased_out.at[p]) for p in parts]
    trips += [(scores, scores_v, scores_out), (cnt, cnt_v, cnt_out)]
    ins = [pltpu.make_async_copy(a, v, sems.at[0, i]) for i, (a, v, _) in enumerate(trips)]
    outs = [pltpu.make_async_copy(v, b, sems.at[1, i]) for i, (_, v, b) in enumerate(trips)]
    for cp in ins:
        cp.start()
    for load, store in zip(ins, outs):
        load.wait()
        store.start()
    for cp in outs:
        cp.wait()


def per_device(acts, mean_vec, left_factor, right_factor, labels, counts):
    dma = pltpu.SemaphoreType.DMA
    ng = len(GROUPS)
    vm, anywhere = pl.BlockSpec(memory_space=pltpu.VMEM), pl.BlockSpec(memory_space=pl.ANY)
    hbm = pl.BlockSpec(memory_space=pltpu.HBM)
    shapes = (
        jax.ShapeDtypeStruct((TOK, D), BF16),
        jax.ShapeDtypeStruct((RD, D), F32),
        jax.ShapeDtypeStruct((1, RD), I32),
    )
    results = pl.pallas_call(
        kernel,
        out_shape=shapes,
        in_specs=[hbm] * 6,
        out_specs=(anywhere, vm, vm),
        scratch_shapes=[
            pltpu.VMEM((1, D), F32),
            pltpu.VMEM((1, TOK), I32),
            pltpu.SMEM((1,), I32),
            pltpu.VMEM((T2, D), BF16),
            pltpu.VMEM((T2, D), BF16),
            pltpu.VMEM((NX, NZ, RD, D), BF16),
            pltpu.VMEM((NX, NZ, RD, D), BF16),
            pltpu.VMEM((NX, NZ, RD, D), BF16),
            pltpu.VMEM((C, D), BF16),
            pltpu.VMEM((2, NX, NZ, 1, TOK), I32),
            pltpu.VMEM((1, TOK), I32),
            pltpu.VMEM((2, T2, K2), BF16),
            pltpu.VMEM((2, NY, YB, K2), BF16),
            pltpu.VMEM((2, 2, T2, K2), BF16),
            pltpu.VMEM((C, T2), BF16),
            pltpu.VMEM((T2, H), BF16),
            pltpu.VMEM((NX, 128, H), BF16),
            pltpu.VMEM((NX, 128, H), BF16),
            pltpu.VMEM((128, H), F32),
            pltpu.VMEM((1, H), F32),
            pltpu.VMEM((NX, 1, H), F32),
            pltpu.VMEM((NZ, 2 * RD, H), BF16),
            pltpu.VMEM((NZ, 2 * RD, H), BF16),
            pltpu.VMEM((1, H), F32),
            pltpu.VMEM((NZ, 1, H), F32),
            pltpu.VMEM((2, M, H), F32),
            pltpu.VMEM((256, D), BF16),
            pltpu.VMEM((NY, M, 256), BF16),
            pltpu.VMEM((2, M, 256), F32),
            pltpu.VMEM((M, 128), F32),
            dma((8,)),
            dma((1,)), dma((ng,)),
            dma((1,)), dma((2,)),
            dma((1,)), dma((1,)),
            dma((1,)), dma((1,)),
            dma((1,)), dma((1,)),
            dma((1,)), dma((1,)),
            dma((8,)), dma((8,)),
            dma((2,)), dma((2,)),
            dma((2,)), dma((2 * NY,)),
            dma((2,)), dma((2,)),
            dma((2,)), dma((2,)),
            dma((2,)), dma((2,)),
            dma((1,)), dma((1,)),
        ],
        compiler_params=pltpu.CompilerParams(
            collective_id=0, has_side_effects=True, vmem_limit_bytes=VLIM
        ),
        cost_estimate=pl.CostEstimate(flops=6 * 256 * 1024 * 512, bytes_accessed=4 << 20, transcendentals=0),
    )(
        acts,
        mean_vec.reshape(1, D),
        left_factor,
        right_factor,
        labels.reshape(1, TOK),
        counts,
    )
    erased, scores, cnt = pl.pallas_call(
        hand_out,
        out_shape=shapes,
        in_specs=[hbm] * 3,
        out_specs=(hbm,) * 3,
        scratch_shapes=[pltpu.VMEM(v.shape, v.dtype) for v in shapes] + [dma((2, PIECES + 2))],
        compiler_params=pltpu.CompilerParams(vmem_limit_bytes=VLIM),
    )(*results)
    return erased, scores, cnt.reshape(RD)


def solution(mesh):
    return jax.shard_map(
        per_device,
        mesh=mesh,
        in_specs=(
            P("dp", "tensor"),
            P("tensor"),
            P("dp", "tensor"),
            P("dp", "tensor"),
            P("dp"),
            P("dp"),
        ),
        out_specs=(P("dp", "tensor"), P("dp", "tensor"), P("dp")),
        check_vma=False,
    )
```

```python
import functools

import jax
import jax.numpy as jnp
from jax import lax
from jax.experimental import pallas as pl
from jax.experimental.pallas import tpu as pltpu
from jax.sharding import PartitionSpec as P

MESH = pl.DeviceIdType.MESH
F32, BF16, I32 = jnp.float32, jnp.bfloat16, jnp.int32
C = 512
NZ, NX, NY = 8, 4, 8
ZORD = (0, 1, 7, 2, 6, 3, 5, 4)
XORD = (0, 1, 3, 2)
ZBACK = tuple(ZORD.index((NZ - d) % NZ) for d in ZORD)
XBACK = tuple(XORD.index((NX - d) % NX) for d in XORD)
NEAR, FAR = (1, 2, 3, 4, 5, 6, 7), (7, 6, 5, 4, 3, 2, 1)
XFIRST = (2, 3, 1)
GROUPS = ((0, 2), (2, 2), (4, 2), (6, 2))
TOK, D, RD = 256, 1024, 8
T2, H, K2 = 512, 512, 128
M = 2 * RD
XW, ZW = 384, 128
YB = T2 // NY
VLIM = 63 << 20
PIECES = 4


def kernel(
    acts, mean, left, right, labels, counts,
    out, scores, cnt,
    meanv, labv, cntv, actv, cen, rg, lg, lo, lm, lab, labo, pbuf, prx, obuf, cbuf, oh, er,
    sxs, sxr, s0, txs, txr, szs, szr, tzs, tzr, fzs, fzr, f0, fxs, fxr, mh, rall, gy, gx, cnts,
    loc, rzs, rzr, rxs, rxr, lzs, lzr, lxs, lxr, bzs, bzr, bxs, bxr, exs, exr,
    pss, psr, css, csr, xxs, xxr, zzs, zzr, ffs, ffr, ggs, ggr,
):
    dp, y = lax.axis_index("dp"), lax.axis_index("tensor")
    c, x, z = lax.rem(dp, 2), lax.rem(dp // 2, NX), dp // (2 * NX)
    oc = 1 - c

    def dev(dz=0, dx=0, dy=0, core=None):
        core = c if core is None else core
        zz, xx, yy = lax.rem(z + dz, NZ), lax.rem(x + dx, NX), lax.rem(y + dy, NY)
        return ((zz * NX + xx) * 2 + core, yy)

    other = dev(core=oc)

    def send(src, dst, ss, rs, to):
        pltpu.make_async_remote_copy(
            src_ref=src,
            dst_ref=dst,
            send_sem=ss[0].at[ss[1]],
            recv_sem=rs[0].at[rs[1]],
            device_id=to,
            device_id_type=MESH,
        ).start()

    def got(ref, rs):
        sem = rs[0].at[rs[1]]
        pltpu.make_async_remote_copy(
            src_ref=ref, dst_ref=ref, send_sem=sem, recv_sem=sem, device_id=other, device_id_type=MESH
        ).wait_recv()

    def gone(ref, ss):
        sem = ss[0].at[ss[1]]
        pltpu.make_async_remote_copy(
            src_ref=ref, dst_ref=ref, send_sem=sem, recv_sem=sem, device_id=other, device_id_type=MESH
        ).wait_send()

    def along_z(order, src, dst, ss, rs):
        for s in order:
            send(src(s), dst(ZBACK[s]), ss, rs(ZBACK[s]), dev(dz=ZORD[s]))

    def along_y(order, src, dst, ss, rs):
        for s in order:
            send(src(s), dst(ZBACK[s]), ss, rs(ZBACK[s]), dev(dy=ZORD[s]))

    def along_x(src, dst, ss, rs):
        for s in XFIRST:
            send(src(s), dst(XBACK[s]), ss, rs(XBACK[s]), dev(dx=XORD[s]))

    mine, theirs = pl.ds(0, TOK), pl.ds(TOK, TOK)
    loads = [
        pltpu.make_async_copy(src, dst, loc.at[i])
        for i, (src, dst) in enumerate(
            (
                (right, rg.at[0, 0]),
                (acts, actv.at[mine]),
                (mean, meanv),
                (labels, labv),
                (counts, cntv),
                (left, lg.at[0, 0]),
            )
        )
    ]
    for cp in loads:
        cp.start()

    barrier = pltpu.get_barrier_semaphore()
    peers = [dev(dz=ZORD[s]) for s in FAR] + [dev(dy=ZORD[s], core=k) for s in FAR for k in (c, oc)]
    peers += [dev(dx=d) for d in (2, 1, 3)] + [other]
    for p in peers:
        pl.semaphore_signal(barrier, inc=1, device_id=p, device_id_type=MESH)
    loads[0].wait()
    pl.semaphore_wait(barrier, len(peers))

    group_of = {s: g for g, (first, number) in enumerate(GROUPS) for s in range(first, first + number)}
    along_z(NEAR, lambda s: rg.at[0, 0], lambda t: rg.at[0, t], (rzs, 0), lambda t: (rzr, group_of[t]))
    loads[1].wait()
    send(actv.at[mine], actv.at[theirs], (exs, 0), (exr, 0), other)
    for cp in loads[2:]:
        cp.wait()
    cen[mine, :] = (actv[mine, :].astype(F32) - meanv[...]).astype(BF16)
    slot_iota = lax.broadcasted_iota(I32, (1, TOK), 1)
    lab[0, 0, 0] = jnp.where(slot_iota < cntv[0], labv[...], -1)
    send(lab.at[0, 0, 0], labo, (exs, 5), (exr, 5), other)

    def right_x(g):
        first, number = GROUPS[g]
        got(rg.at[0, max(first, 1) : first + number], (rzr, g))
        zs = pl.ds(first, number)
        along_x(lambda s: rg.at[0, zs], lambda t: rg.at[t, zs], (rxs, 0), lambda t: (rxr, first // 4))

    half, their_half = pl.ds(pl.multiple_of(c * H, H), H), pl.ds(pl.multiple_of(oc * H, H), H)
    right_x(0)
    right_x(1)
    got(labo, (exr, 5))
    tokens = jnp.concatenate([lab[0, 0, 0], labo[...]], axis=1)
    for xs in range(NX):
        for zs in range(NZ):
            r = lax.broadcasted_iota(I32, (2 * RD, T2), 0)
            owner = lax.rem(z + ZORD[zs], NZ) * NX + lax.rem(x + XORD[xs], NX)
            at = (xs * NZ + zs) * 2 * RD
            oh[at : at + 2 * RD, :] = (owner * (2 * RD) + r == tokens).astype(F32).astype(BF16)
    got(actv.at[theirs], (exr, 0))
    cen[theirs, :] = (actv[theirs, :].astype(F32) - meanv[...]).astype(BF16)
    sums = jnp.dot(oh[...], actv[:, half], preferred_element_type=F32)
    for zs in range(NZ):
        for xs in range(NX):
            at = (xs * NZ + zs) * M
            part = sums[at : at + M, XW:]
            if zs:
                fzs[zs, xs * M : (xs + 1) * M, :] = part.astype(BF16)
            else:
                f0[xs * M : (xs + 1) * M, :] = part
    along_z(NEAR, lambda s: fzs.at[s], lambda t: fzr.at[t], (ffs, 0), lambda t: (ffr, 0))
    s0[...] = sums[:128, :XW]
    txs[...] = jnp.sum(sums, axis=0, keepdims=True)
    for s in range(1, NX):
        sxs[s] = sums[s * 128 : (s + 1) * 128, :XW].astype(BF16)
    along_x(lambda s: sxs.at[s], lambda t: sxr.at[t], (xxs, 0), lambda t: (xxr, 0))
    along_x(lambda s: txs, lambda t: txr.at[t], (xxs, 1), lambda t: (xxr, 1))
    right_x(2)
    right_x(3)
    along_z(NEAR, lambda s: lab.at[0, 0, 0], lambda t: lab.at[0, 0, t], (bzs, 0), lambda t: (bzr, 0))

    def block(s):
        return pl.ds(pl.multiple_of(lax.rem(y + ZORD[s], NY) * YB, YB), YB)

    def chunk(k):
        got(rg.at[1:NX, 4 * k : 4 * k + 4], (rxr, k))
        rmat = rg[:, 4 * k : 4 * k + 4].astype(F32).reshape(K2, D).astype(BF16)
        rall[k * K2 : (k + 1) * K2, :] = rmat
        part = lax.dot_general(cen[...], rmat, (((1,), (1,)), ((), ())), preferred_element_type=F32)
        pbuf[k] = part.astype(BF16)
        along_y(FAR, lambda s: pbuf.at[k, block(s)], lambda t: prx.at[k, t], (pss, k), lambda t: (psr, k))

    near_half = y < NY // 2
    taker = lax.rem(c + y // (NY // 2), 2)

    def reduce(k):
        total = pbuf[k, block(0), :].astype(F32)
        got(prx.at[k, 1:NY], (psr, k))
        for s in range(1, NY):
            total = total + prx[k, s].astype(F32)
        obuf[k] = total.astype(BF16)
        there = cbuf.at[k, block(0)]
        for s in FAR:
            send(obuf.at[k], there, (css, k), (csr, k), dev(dy=ZORD[s], core=taker))

        @pl.when(near_half)
        def _():
            there[...] = obuf[k]

        @pl.when(jnp.logical_not(near_half))
        def _():
            send(obuf.at[k], there, (css, k), (csr, k), other)

    def gathered(k):
        @pl.when(near_half)
        def _():
            got(cbuf.at[k, 0 : T2 - YB], (csr, k))

        @pl.when(jnp.logical_not(near_half))
        def _():
            got(cbuf.at[k], (csr, k))

    along_z(NEAR, lambda s: lg.at[0, 0], lambda t: lg.at[0, t], (lzs, 0), lambda t: (lzr, 0))
    chunk(0)
    got(lab.at[0, 0, 1:NZ], (bzr, 0))
    along_x(lambda s: lab.at[0, 0], lambda t: lab.at[0, t], (bxs, 0), lambda t: (bxr, 0))
    chunk(1)
    got(lg.at[0, 1:NZ], (lzr, 0))
    along_x(lambda s: lg.at[0], lambda t: lg.at[t], (lxs, 0), lambda t: (lxr, 0))
    got(lab.at[0, 1:NX], (bxr, 0))
    send(lab.at[0], lab.at[1], (exs, 1), (exr, 1), other)

    total = s0[...]
    got(sxr.at[1:NX], (xxr, 0))
    for s in range(1, NX):
        total = total + sxr[s].astype(F32)
    for s in NEAR:
        szs[s] = total[s * 2 * RD : (s + 1) * 2 * RD, :].astype(BF16)
    mh[0, :, 0:XW] = total[0:M]
    along_z(FAR, lambda s: szs.at[s], lambda t: szr.at[t], (zzs, 0), lambda t: (zzr, 0))
    total = txs[...]
    got(txr.at[1:NX], (xxr, 1))
    for s in range(1, NX):
        total = total + txr[s]
    tzs[...] = total
    along_z(FAR, lambda s: tzs, lambda t: tzr.at[t], (zzs, 1), lambda t: (zzr, 1))
    total = f0[...]
    got(fzr.at[1:NZ], (ffr, 0))
    for s in range(1, NZ):
        total = total + fzr[s].astype(F32)
    mh[0, :, XW:] = total[0:M]
    for s in range(1, NX):
        fxs[s] = total[s * M : (s + 1) * M, :].astype(BF16)
    along_x(lambda s: fxs.at[s], lambda t: fxr.at[t], (ffs, 1), lambda t: (ffr, 1))
    reduce(0)
    reduce(1)

    got(lab.at[1], (exr, 1))
    chip = z * NX + x
    own_class = chip * (2 * RD) + lax.broadcasted_iota(I32, (2 * RD, TOK), 0)
    hits, valid = jnp.zeros((2 * RD, TOK), F32), jnp.zeros((1, TOK), F32)
    for k in range(2):
        for xs in range(NX):
            for zs in range(NZ):
                row = lab[k, xs, zs]
                hits = hits + (row == own_class).astype(F32)
                valid = valid + (row >= 0).astype(F32)
    own_counts = jnp.sum(hits, axis=1, keepdims=True)
    grand = jnp.sum(valid, axis=1, keepdims=True)

    got(lg.at[1:NX], (lxr, 0))
    send(lg, lo, (exs, 2), (exr, 2), other)
    for k in range(2):
        lm[k * K2 : (k + 1) * K2, :] = lg[:, 4 * k : 4 * k + 4].astype(F32).reshape(K2, D).astype(BF16)
    got(szr.at[1:NZ], (zzr, 0))
    got(tzr.at[1:NZ], (zzr, 1))
    first_sums, other_sums, total = mh[0, :, 0:XW], mh[0, :, XW:], tzs[...]
    for s in range(1, NZ):
        first_sums = first_sums + szr[s].astype(F32)
        total = total + tzr[s]
    got(fxr.at[1:NX], (ffr, 1))
    for s in range(1, NX):
        other_sums = other_sums + fxr[s].astype(F32)
    mean_act = total / grand
    mh[0, :, 0:XW] = first_sums - own_counts * mean_act[:, 0:XW]
    mh[0, :, XW:] = other_sums - own_counts * mean_act[:, XW:]
    send(mh.at[0], mh.at[1], (exs, 6), (exr, 6), other)

    def twice(a, b, dims):
        high = a.astype(BF16).astype(F32)
        terms = jnp.concatenate([high, a - high], axis=0).astype(BF16)
        both = lax.dot_general(terms, b, (dims, ((), ())), preferred_element_type=F32)
        return both[: a.shape[0]] + both[a.shape[0] :]

    got(mh.at[1], (exr, 6))
    gsum = twice(mh[0], rall[:, half], ((1,), (1,))) + twice(mh[1], rall[:, their_half], ((1,), (1,)))
    gy[0] = gsum.astype(BF16)
    along_y(FAR, lambda s: gy.at[0], lambda t: gy.at[t], (ggs, 0), lambda t: (ggr, 0))

    got(lo, (exr, 2))
    for k in range(2, 4):
        lm[k * K2 : (k + 1) * K2, :] = lo[:, 4 * k - 8 : 4 * k - 4].astype(F32).reshape(K2, D).astype(BF16)
    gathered(0)
    gathered(1)

    coords = jnp.concatenate([cbuf[0, 0:TOK], cbuf[1, 0:TOK], cbuf[0, TOK:T2], cbuf[1, TOK:T2]], axis=1)
    keeps = []
    for q in range(2):
        cols = pl.ds(q * H, H)
        corr = jnp.dot(coords, lm[:, cols], preferred_element_type=F32)
        er[:, cols] = (actv[mine, cols].astype(F32) - corr).astype(BF16)
        keeps.append(pltpu.make_async_copy(er.at[:, cols], out.at[:, cols], loc.at[6 + q]))
        keeps[q].start()

    got(gy.at[1:NY], (ggr, 0))
    for s in range(1, NY):
        gsum = gsum + gy[s].astype(F32)
    gx[0] = gsum
    ours, others = pl.ds(pl.multiple_of(c * RD, RD), RD), pl.ds(pl.multiple_of(oc * RD, RD), RD)
    send(gx.at[0, others], gx.at[1, others], (exs, 7), (exr, 7), other)
    cnts[...] = jnp.broadcast_to(own_counts, (M, 128))
    own_counts = cnts[ours, 0:1]
    lane = lax.broadcasted_iota(I32, (RD, RD), 1)
    row = lax.broadcasted_iota(I32, (RD, RD), 0)
    cnt[...] = jnp.sum(jnp.where(lane == row, own_counts, 0.0), axis=0, keepdims=True).astype(I32)
    scale = 1.0 / jnp.sqrt(jnp.maximum(own_counts, 1.0))
    got(gx.at[1, ours], (exr, 7))
    coords = jnp.concatenate([gx[0, ours, :], gx[1, ours, :]], axis=1)
    moved = twice(coords, lm[...], ((1,), (0,)))
    scores[...] = moved * -scale
    for k, cols in enumerate((half, their_half)):
        scores[:, cols] += mh[k, ours, :] * scale

    for cp in keeps:
        cp.wait()
    gone(rg.at[0, 1:NZ], (rzs, 0))
    gone(rg.at[1:NX], (rxs, 0))
    gone(lab.at[0, 0, 1:NZ], (bzs, 0))
    gone(lg.at[0, 1:NZ], (lzs, 0))
    gone(lab.at[0, 1:NX], (bxs, 0))
    gone(lg.at[1:NX], (lxs, 0))
    gone(actv.at[mine], (exs, 0))
    gone(lab.at[0], (exs, 1))
    gone(lo, (exs, 2))
    for k in range(2):
        gone(prx.at[k, 1:NY], (pss, k))
    gone(sxr.at[1:NX], (xxs, 0))
    gone(szr.at[1:NZ], (zzs, 0))
    gone(txr.at[1:NX], (xxs, 1))
    gone(tzr.at[1:NZ], (zzs, 1))

    @pl.when(near_half)
    def _():
        for k in range(2):
            gone(cbuf.at[k, 0 : T2 - YB], (css, k))

    @pl.when(jnp.logical_not(near_half))
    def _():
        for k in range(2):
            gone(cbuf.at[k], (css, k))

    gone(fzr.at[1:NZ], (ffs, 0))
    gone(fxr.at[1:NX], (ffs, 1))
    gone(gy.at[1:NY], (ggs, 0))
    gone(labo, (exs, 5))
    gone(mh.at[0], (exs, 6))
    gone(gx.at[0, others], (exs, 7))


def hand_out(erased, scores, cnt, erased_out, scores_out, cnt_out, erased_v, scores_v, cnt_v, sems):
    rows = TOK // PIECES
    parts = [pl.ds(i * rows, rows) for i in range(PIECES)]
    trips = [(erased.at[p], erased_v.at[p], erased_out.at[p]) for p in parts]
    trips += [(scores, scores_v, scores_out), (cnt, cnt_v, cnt_out)]
    ins = [pltpu.make_async_copy(a, v, sems.at[0, i]) for i, (a, v, _) in enumerate(trips)]
    outs = [pltpu.make_async_copy(v, b, sems.at[1, i]) for i, (_, v, b) in enumerate(trips)]
    for cp in ins:
        cp.start()
    for load, store in zip(ins, outs):
        load.wait()
        store.start()
    for cp in outs:
        cp.wait()


def per_device(acts, mean_vec, left_factor, right_factor, labels, counts):
    dma = pltpu.SemaphoreType.DMA
    ng = len(GROUPS)
    vm, anywhere = pl.BlockSpec(memory_space=pltpu.VMEM), pl.BlockSpec(memory_space=pl.ANY)
    hbm = pl.BlockSpec(memory_space=pltpu.HBM)
    shapes = (
        jax.ShapeDtypeStruct((TOK, D), BF16),
        jax.ShapeDtypeStruct((RD, D), F32),
        jax.ShapeDtypeStruct((1, RD), I32),
    )
    results = pl.pallas_call(
        kernel,
        out_shape=shapes,
        in_specs=[hbm] * 6,
        out_specs=(anywhere, vm, vm),
        scratch_shapes=[
            pltpu.VMEM((1, D), F32),
            pltpu.VMEM((1, TOK), I32),
            pltpu.SMEM((1,), I32),
            pltpu.VMEM((T2, D), BF16),
            pltpu.VMEM((T2, D), BF16),
            pltpu.VMEM((NX, NZ, RD, D), BF16),
            pltpu.VMEM((NX, NZ, RD, D), BF16),
            pltpu.VMEM((NX, NZ, RD, D), BF16),
            pltpu.VMEM((C, D), BF16),
            pltpu.VMEM((2, NX, NZ, 1, TOK), I32),
            pltpu.VMEM((1, TOK), I32),
            pltpu.VMEM((2, T2, K2), BF16),
            pltpu.VMEM((2, NY, YB, K2), BF16),
            pltpu.VMEM((2, YB, K2), BF16),
            pltpu.VMEM((2, T2, K2), BF16),
            pltpu.VMEM((C, T2), BF16),
            pltpu.VMEM((TOK, D), BF16),
            pltpu.VMEM((NX, 128, XW), BF16),
            pltpu.VMEM((NX, 128, XW), BF16),
            pltpu.VMEM((128, XW), F32),
            pltpu.VMEM((1, H), F32),
            pltpu.VMEM((NX, 1, H), F32),
            pltpu.VMEM((NZ, M, XW), BF16),
            pltpu.VMEM((NZ, M, XW), BF16),
            pltpu.VMEM((1, H), F32),
            pltpu.VMEM((NZ, 1, H), F32),
            pltpu.VMEM((NZ, NX * M, ZW), BF16),
            pltpu.VMEM((NZ, NX * M, ZW), BF16),
            pltpu.VMEM((NX * M, ZW), F32),
            pltpu.VMEM((NX, M, ZW), BF16),
            pltpu.VMEM((NX, M, ZW), BF16),
            pltpu.VMEM((2, M, H), F32),
            pltpu.VMEM((256, D), BF16),
            pltpu.VMEM((NY, M, 256), BF16),
            pltpu.VMEM((2, M, 256), F32),
            pltpu.VMEM((M, 128), F32),
            dma((8,)),
            dma((1,)), dma((ng,)),
            dma((1,)), dma((2,)),
            dma((1,)), dma((1,)),
            dma((1,)), dma((1,)),
            dma((1,)), dma((1,)),
            dma((1,)), dma((1,)),
            dma((8,)), dma((8,)),
            dma((2,)), dma((2,)),
            dma((2,)), dma((2,)),
            dma((2,)), dma((2,)),
            dma((2,)), dma((2,)),
            dma((2,)), dma((2,)),
            dma((1,)), dma((1,)),
        ],
        compiler_params=pltpu.CompilerParams(
            collective_id=0, has_side_effects=True, vmem_limit_bytes=VLIM
        ),
        cost_estimate=pl.CostEstimate(flops=6 * 256 * 1024 * 512, bytes_accessed=4 << 20, transcendentals=0),
    )(
        acts,
        mean_vec.reshape(1, D),
        left_factor,
        right_factor,
        labels.reshape(1, TOK),
        counts,
    )
    erased, scores, cnt = pl.pallas_call(
        hand_out,
        out_shape=shapes,
        in_specs=[hbm] * 3,
        out_specs=(hbm,) * 3,
        scratch_shapes=[pltpu.VMEM(v.shape, v.dtype) for v in shapes] + [dma((2, PIECES + 2))],
        compiler_params=pltpu.CompilerParams(vmem_limit_bytes=VLIM),
    )(*results)
    return erased, scores, cnt.reshape(RD)


def solution(mesh):
    return jax.shard_map(
        per_device,
        mesh=mesh,
        in_specs=(
            P("dp", "tensor"),
            P("tensor"),
            P("dp", "tensor"),
            P("dp", "tensor"),
            P("dp"),
            P("dp"),
        ),
        out_specs=(P("dp", "tensor"), P("dp", "tensor"), P("dp")),
        check_vma=False,
    )
```

```python
import functools

import jax
import jax.numpy as jnp
from jax import lax
from jax.experimental import pallas as pl
from jax.experimental.pallas import tpu as pltpu
from jax.sharding import PartitionSpec as P

MESH = pl.DeviceIdType.MESH
F32, BF16, I32 = jnp.float32, jnp.bfloat16, jnp.int32
C = 512
NZ, NX, NY = 8, 4, 8
ZORD = (0, 1, 7, 2, 6, 3, 5, 4)
XORD = (0, 1, 3, 2)
ZBACK = tuple(ZORD.index((NZ - d) % NZ) for d in ZORD)
XBACK = tuple(XORD.index((NX - d) % NX) for d in XORD)
NEAR, FAR = (1, 2, 3, 4, 5, 6, 7), (7, 6, 5, 4, 3, 2, 1)
XFIRST = (2, 3, 1)
GROUPS = ((0, 2), (2, 2), (4, 2), (6, 2))
TOK, D, RD = 256, 1024, 8
T2, H, K2 = 512, 512, 128
M = 2 * RD
XW, ZW = 384, 128
YB = T2 // NY
VLIM = 40 << 20
PIECES = 4


def kernel(
    acts, mean, left, right, labels, counts,
    out, scores, cnt,
    meanv, labv, cntv, actv, cen, rg, lg, lo, lm, lab, labo, pbuf, prx, obuf, cbuf, oh, er,
    sxs, sxr, s0, txs, txr, szs, szr, tzs, tzr, fzs, fzr, f0, fxs, fxr, mh, rall, gy, gx, cnts,
    loc, rzs, rzr, rxs, rxr, lzs, lzr, lxs, lxr, bzs, bzr, bxs, bxr, exs, exr,
    pss, psr, css, csr, xxs, xxr, zzs, zzr, ffs, ffr, ggs, ggr,
):
    dp, y = lax.axis_index("dp"), lax.axis_index("tensor")
    c, x, z = lax.rem(dp, 2), lax.rem(dp // 2, NX), dp // (2 * NX)
    oc = 1 - c

    def dev(dz=0, dx=0, dy=0, core=None):
        core = c if core is None else core
        zz, xx, yy = lax.rem(z + dz, NZ), lax.rem(x + dx, NX), lax.rem(y + dy, NY)
        return ((zz * NX + xx) * 2 + core, yy)

    other = dev(core=oc)

    def send(src, dst, ss, rs, to):
        pltpu.make_async_remote_copy(
            src_ref=src,
            dst_ref=dst,
            send_sem=ss[0].at[ss[1]],
            recv_sem=rs[0].at[rs[1]],
            device_id=to,
            device_id_type=MESH,
        ).start()

    def got(ref, rs):
        sem = rs[0].at[rs[1]]
        pltpu.make_async_remote_copy(
            src_ref=ref, dst_ref=ref, send_sem=sem, recv_sem=sem, device_id=other, device_id_type=MESH
        ).wait_recv()

    def gone(ref, ss):
        sem = ss[0].at[ss[1]]
        pltpu.make_async_remote_copy(
            src_ref=ref, dst_ref=ref, send_sem=sem, recv_sem=sem, device_id=other, device_id_type=MESH
        ).wait_send()

    def along_z(order, src, dst, ss, rs):
        for s in order:
            send(src(s), dst(ZBACK[s]), ss, rs(ZBACK[s]), dev(dz=ZORD[s]))

    def along_y(order, src, dst, ss, rs):
        for s in order:
            send(src(s), dst(ZBACK[s]), ss, rs(ZBACK[s]), dev(dy=ZORD[s]))

    def along_x(src, dst, ss, rs):
        for s in XFIRST:
            send(src(s), dst(XBACK[s]), ss, rs(XBACK[s]), dev(dx=XORD[s]))

    mine, theirs = pl.ds(0, TOK), pl.ds(TOK, TOK)
    loads = [
        pltpu.make_async_copy(src, dst, loc.at[i])
        for i, (src, dst) in enumerate(
            (
                (right, rg.at[0, 0]),
                (acts, actv.at[mine]),
                (mean, meanv),
                (labels, labv),
                (counts, cntv),
                (left, lg.at[0, 0]),
            )
        )
    ]
    for cp in loads:
        cp.start()

    barrier = pltpu.get_barrier_semaphore()
    peers = [dev(dz=ZORD[s]) for s in FAR] + [dev(dy=ZORD[s]) for s in FAR]
    peers += [dev(dx=d) for d in (2, 1, 3)] + [other]
    for p in peers:
        pl.semaphore_signal(barrier, inc=1, device_id=p, device_id_type=MESH)
    loads[0].wait()
    pl.semaphore_wait(barrier, len(peers))

    group_of = {s: g for g, (first, number) in enumerate(GROUPS) for s in range(first, first + number)}
    along_z(NEAR, lambda s: rg.at[0, 0], lambda t: rg.at[0, t], (rzs, 0), lambda t: (rzr, group_of[t]))
    loads[1].wait()
    send(actv.at[mine], actv.at[theirs], (exs, 0), (exr, 0), other)
    for cp in loads[2:]:
        cp.wait()
    cen[mine, :] = (actv[mine, :].astype(F32) - meanv[...]).astype(BF16)
    slot_iota = lax.broadcasted_iota(I32, (1, TOK), 1)
    lab[0, 0, 0] = jnp.where(slot_iota < cntv[0], labv[...], -1)
    send(lab.at[0, 0, 0], labo, (exs, 5), (exr, 5), other)

    def right_x(g):
        first, number = GROUPS[g]
        got(rg.at[0, max(first, 1) : first + number], (rzr, g))
        zs = pl.ds(first, number)
        along_x(lambda s: rg.at[0, zs], lambda t: rg.at[t, zs], (rxs, 0), lambda t: (rxr, first // 4))

    half, their_half = pl.ds(pl.multiple_of(c * H, H), H), pl.ds(pl.multiple_of(oc * H, H), H)
    right_x(0)
    right_x(1)
    got(labo, (exr, 5))
    tokens = jnp.concatenate([lab[0, 0, 0], labo[...]], axis=1)
    for xs in range(NX):
        for zs in range(NZ):
            r = lax.broadcasted_iota(I32, (2 * RD, T2), 0)
            owner = lax.rem(z + ZORD[zs], NZ) * NX + lax.rem(x + XORD[xs], NX)
            at = (xs * NZ + zs) * 2 * RD
            oh[at : at + 2 * RD, :] = (owner * (2 * RD) + r == tokens).astype(F32).astype(BF16)
    got(actv.at[theirs], (exr, 0))
    cen[theirs, :] = (actv[theirs, :].astype(F32) - meanv[...]).astype(BF16)
    sums = jnp.dot(oh[...], actv[:, half], preferred_element_type=F32)
    for zs in range(NZ):
        for xs in range(NX):
            at = (xs * NZ + zs) * M
            part = sums[at : at + M, XW:]
            if zs:
                fzs[zs, xs * M : (xs + 1) * M, :] = part.astype(BF16)
            else:
                f0[xs * M : (xs + 1) * M, :] = part
    along_z(NEAR, lambda s: fzs.at[s], lambda t: fzr.at[t], (ffs, 0), lambda t: (ffr, 0))
    s0[...] = sums[:128, :XW]
    txs[...] = jnp.sum(sums, axis=0, keepdims=True)
    for s in range(1, NX):
        sxs[s] = sums[s * 128 : (s + 1) * 128, :XW].astype(BF16)
    along_x(lambda s: sxs.at[s], lambda t: sxr.at[t], (xxs, 0), lambda t: (xxr, 0))
    along_x(lambda s: txs, lambda t: txr.at[t], (xxs, 1), lambda t: (xxr, 1))
    right_x(2)
    right_x(3)
    along_z(NEAR, lambda s: lab.at[0, 0, 0], lambda t: lab.at[0, 0, t], (bzs, 0), lambda t: (bzr, 0))

    def block(s):
        return pl.ds(pl.multiple_of(lax.rem(y + ZORD[s], NY) * YB, YB), YB)

    def chunk(k):
        got(rg.at[1:NX, 4 * k : 4 * k + 4], (rxr, k))
        rmat = rg[:, 4 * k : 4 * k + 4].astype(F32).reshape(K2, D).astype(BF16)
        rall[k * K2 : (k + 1) * K2, :] = rmat
        part = lax.dot_general(cen[...], rmat, (((1,), (1,)), ((), ())), preferred_element_type=F32)
        pbuf[k] = part.astype(BF16)
        along_y(FAR, lambda s: pbuf.at[k, block(s)], lambda t: prx.at[k, t], (pss, k), lambda t: (psr, k))

    near_half = y < NY // 2
    taker = lax.rem(c + y // (NY // 2), 2)

    def reduce(k):
        total = pbuf[k, block(0), :].astype(F32)
        got(prx.at[k, 1:NY], (psr, k))
        for s in range(1, NY):
            total = total + prx[k, s].astype(F32)
        obuf[k] = total.astype(BF16)
        there = cbuf.at[k, block(0)]
        for s in FAR:
            send(obuf.at[k], there, (css, k), (csr, k), dev(dy=ZORD[s], core=taker))

        @pl.when(near_half)
        def _():
            there[...] = obuf[k]

        @pl.when(jnp.logical_not(near_half))
        def _():
            send(obuf.at[k], there, (css, k), (csr, k), other)

    def gathered(k):
        @pl.when(near_half)
        def _():
            got(cbuf.at[k, 0 : T2 - YB], (csr, k))

        @pl.when(jnp.logical_not(near_half))
        def _():
            got(cbuf.at[k], (csr, k))

    along_z(NEAR, lambda s: lg.at[0, 0], lambda t: lg.at[0, t], (lzs, 0), lambda t: (lzr, 0))
    chunk(0)
    got(lab.at[0, 0, 1:NZ], (bzr, 0))
    along_x(lambda s: lab.at[0, 0], lambda t: lab.at[0, t], (bxs, 0), lambda t: (bxr, 0))
    chunk(1)
    got(lg.at[0, 1:NZ], (lzr, 0))
    along_x(lambda s: lg.at[0], lambda t: lg.at[t], (lxs, 0), lambda t: (lxr, 0))
    got(lab.at[0, 1:NX], (bxr, 0))
    send(lab.at[0], lab.at[1], (exs, 1), (exr, 1), other)

    total = s0[...]
    got(sxr.at[1:NX], (xxr, 0))
    for s in range(1, NX):
        total = total + sxr[s].astype(F32)
    for s in NEAR:
        szs[s] = total[s * 2 * RD : (s + 1) * 2 * RD, :].astype(BF16)
    mh[0, :, 0:XW] = total[0:M]
    along_z(FAR, lambda s: szs.at[s], lambda t: szr.at[t], (zzs, 0), lambda t: (zzr, 0))
    total = txs[...]
    got(txr.at[1:NX], (xxr, 1))
    for s in range(1, NX):
        total = total + txr[s]
    tzs[...] = total
    along_z(FAR, lambda s: tzs, lambda t: tzr.at[t], (zzs, 1), lambda t: (zzr, 1))
    total = f0[...]
    got(fzr.at[1:NZ], (ffr, 0))
    for s in range(1, NZ):
        total = total + fzr[s].astype(F32)
    mh[0, :, XW:] = total[0:M]
    for s in range(1, NX):
        fxs[s] = total[s * M : (s + 1) * M, :].astype(BF16)
    along_x(lambda s: fxs.at[s], lambda t: fxr.at[t], (ffs, 1), lambda t: (ffr, 1))
    reduce(0)
    reduce(1)

    got(lab.at[1], (exr, 1))
    chip = z * NX + x
    own_class = chip * (2 * RD) + lax.broadcasted_iota(I32, (2 * RD, TOK), 0)
    hits, valid = jnp.zeros((2 * RD, TOK), F32), jnp.zeros((1, TOK), F32)
    for k in range(2):
        for xs in range(NX):
            for zs in range(NZ):
                row = lab[k, xs, zs]
                hits = hits + (row == own_class).astype(F32)
                valid = valid + (row >= 0).astype(F32)
    own_counts = jnp.sum(hits, axis=1, keepdims=True)
    grand = jnp.sum(valid, axis=1, keepdims=True)

    got(szr.at[1:NZ], (zzr, 0))
    got(tzr.at[1:NZ], (zzr, 1))
    first_sums, other_sums, total = mh[0, :, 0:XW], mh[0, :, XW:], tzs[...]
    for s in range(1, NZ):
        first_sums = first_sums + szr[s].astype(F32)
        total = total + tzr[s]
    got(fxr.at[1:NX], (ffr, 1))
    for s in range(1, NX):
        other_sums = other_sums + fxr[s].astype(F32)
    mean_act = total / grand
    mh[0, :, 0:XW] = first_sums - own_counts * mean_act[:, 0:XW]
    mh[0, :, XW:] = other_sums - own_counts * mean_act[:, XW:]
    send(mh.at[0], mh.at[1], (exs, 6), (exr, 6), other)

    def twice(a, b, dims):
        high = a.astype(BF16).astype(F32)
        terms = jnp.concatenate([high, a - high], axis=0).astype(BF16)
        both = lax.dot_general(terms, b, (dims, ((), ())), preferred_element_type=F32)
        return both[: a.shape[0]] + both[a.shape[0] :]

    got(mh.at[1], (exr, 6))
    gsum = twice(mh[0], rall[:, half], ((1,), (1,))) + twice(mh[1], rall[:, their_half], ((1,), (1,)))
    gy[0] = gsum.astype(BF16)
    along_y(FAR, lambda s: gy.at[0], lambda t: gy.at[t], (ggs, 0), lambda t: (ggr, 0))

    got(lg.at[1:NX], (lxr, 0))
    send(lg, lo, (exs, 2), (exr, 2), other)
    for k in range(2):
        lm[k * K2 : (k + 1) * K2, :] = lg[:, 4 * k : 4 * k + 4].astype(F32).reshape(K2, D).astype(BF16)
    got(lo, (exr, 2))
    for k in range(2, 4):
        lm[k * K2 : (k + 1) * K2, :] = lo[:, 4 * k - 8 : 4 * k - 4].astype(F32).reshape(K2, D).astype(BF16)
    gathered(0)
    gathered(1)

    coords = jnp.concatenate([cbuf[0, 0:TOK], cbuf[1, 0:TOK], cbuf[0, TOK:T2], cbuf[1, TOK:T2]], axis=1)
    keeps = []
    for q in range(2):
        cols = pl.ds(q * H, H)
        corr = jnp.dot(coords, lm[:, cols], preferred_element_type=F32)
        er[:, cols] = (actv[mine, cols].astype(F32) - corr).astype(BF16)
        keeps.append(pltpu.make_async_copy(er.at[:, cols], out.at[:, cols], loc.at[6 + q]))
        keeps[q].start()

    got(gy.at[1:NY], (ggr, 0))
    for s in range(1, NY):
        gsum = gsum + gy[s].astype(F32)
    gx[0] = gsum
    ours, others = pl.ds(pl.multiple_of(c * RD, RD), RD), pl.ds(pl.multiple_of(oc * RD, RD), RD)
    send(gx.at[0, others], gx.at[1, others], (exs, 7), (exr, 7), other)
    cnts[...] = jnp.broadcast_to(own_counts, (M, 128))
    own_counts = cnts[ours, 0:1]
    lane = lax.broadcasted_iota(I32, (RD, RD), 1)
    row = lax.broadcasted_iota(I32, (RD, RD), 0)
    cnt[...] = jnp.sum(jnp.where(lane == row, own_counts, 0.0), axis=0, keepdims=True).astype(I32)
    scale = 1.0 / jnp.sqrt(jnp.maximum(own_counts, 1.0))
    got(gx.at[1, ours], (exr, 7))
    coords = jnp.concatenate([gx[0, ours, :], gx[1, ours, :]], axis=1)
    moved = twice(coords, lm[...], ((1,), (0,)))
    scores[...] = moved * -scale
    for k, cols in enumerate((half, their_half)):
        scores[:, cols] += mh[k, ours, :] * scale

    for cp in keeps:
        cp.wait()
    gone(rg.at[0, 1:NZ], (rzs, 0))
    gone(rg.at[1:NX], (rxs, 0))
    gone(lab.at[0, 0, 1:NZ], (bzs, 0))
    gone(lg.at[0, 1:NZ], (lzs, 0))
    gone(lab.at[0, 1:NX], (bxs, 0))
    gone(lg.at[1:NX], (lxs, 0))
    gone(actv.at[mine], (exs, 0))
    gone(lab.at[0], (exs, 1))
    gone(lo, (exs, 2))
    for k in range(2):
        gone(prx.at[k, 1:NY], (pss, k))
    gone(sxr.at[1:NX], (xxs, 0))
    gone(szr.at[1:NZ], (zzs, 0))
    gone(txr.at[1:NX], (xxs, 1))
    gone(tzr.at[1:NZ], (zzs, 1))

    @pl.when(near_half)
    def _():
        for k in range(2):
            gone(cbuf.at[k, 0 : T2 - YB], (css, k))

    @pl.when(jnp.logical_not(near_half))
    def _():
        for k in range(2):
            gone(cbuf.at[k], (css, k))

    gone(fzr.at[1:NZ], (ffs, 0))
    gone(fxr.at[1:NX], (ffs, 1))
    gone(gy.at[1:NY], (ggs, 0))
    gone(labo, (exs, 5))
    gone(mh.at[0], (exs, 6))
    gone(gx.at[0, others], (exs, 7))


def hand_out(erased, scores, cnt, erased_out, scores_out, cnt_out, sems):
    pairs = ((erased, erased_out), (scores, scores_out), (cnt, cnt_out))
    copies = [pltpu.make_async_copy(a, b, sems.at[i]) for i, (a, b) in enumerate(pairs)]
    for cp in copies:
        cp.start()
    for cp in copies:
        cp.wait()


def per_device(acts, mean_vec, left_factor, right_factor, labels, counts):
    dma = pltpu.SemaphoreType.DMA
    ng = len(GROUPS)
    vm, anywhere = pl.BlockSpec(memory_space=pltpu.VMEM), pl.BlockSpec(memory_space=pl.ANY)
    hbm = pl.BlockSpec(memory_space=pltpu.HBM)
    shapes = (
        jax.ShapeDtypeStruct((TOK, D), BF16),
        jax.ShapeDtypeStruct((RD, D), F32),
        jax.ShapeDtypeStruct((1, RD), I32),
    )
    results = pl.pallas_call(
        kernel,
        out_shape=tuple(pltpu.VMEM(v.shape, v.dtype) for v in shapes),
        in_specs=[hbm] * 6,
        scratch_shapes=[
            pltpu.VMEM((1, D), F32),
            pltpu.VMEM((1, TOK), I32),
            pltpu.SMEM((1,), I32),
            pltpu.VMEM((T2, D), BF16),
            pltpu.VMEM((T2, D), BF16),
            pltpu.VMEM((NX, NZ, RD, D), BF16),
            pltpu.VMEM((NX, NZ, RD, D), BF16),
            pltpu.VMEM((NX, NZ, RD, D), BF16),
            pltpu.VMEM((C, D), BF16),
            pltpu.VMEM((2, NX, NZ, 1, TOK), I32),
            pltpu.VMEM((1, TOK), I32),
            pltpu.VMEM((2, T2, K2), BF16),
            pltpu.VMEM((2, NY, YB, K2), BF16),
            pltpu.VMEM((2, YB, K2), BF16),
            pltpu.VMEM((2, T2, K2), BF16),
            pltpu.VMEM((C, T2), BF16),
            pltpu.VMEM((TOK, D), BF16),
            pltpu.VMEM((NX, 128, XW), BF16),
            pltpu.VMEM((NX, 128, XW), BF16),
            pltpu.VMEM((128, XW), F32),
            pltpu.VMEM((1, H), F32),
            pltpu.VMEM((NX, 1, H), F32),
            pltpu.VMEM((NZ, M, XW), BF16),
            pltpu.VMEM((NZ, M, XW), BF16),
            pltpu.VMEM((1, H), F32),
            pltpu.VMEM((NZ, 1, H), F32),
            pltpu.VMEM((NZ, NX * M, ZW), BF16),
            pltpu.VMEM((NZ, NX * M, ZW), BF16),
            pltpu.VMEM((NX * M, ZW), F32),
            pltpu.VMEM((NX, M, ZW), BF16),
            pltpu.VMEM((NX, M, ZW), BF16),
            pltpu.VMEM((2, M, H), F32),
            pltpu.VMEM((256, D), BF16),
            pltpu.VMEM((NY, M, 256), BF16),
            pltpu.VMEM((2, M, 256), F32),
            pltpu.VMEM((M, 128), F32),
            dma((8,)),
            dma((1,)), dma((ng,)),
            dma((1,)), dma((2,)),
            dma((1,)), dma((1,)),
            dma((1,)), dma((1,)),
            dma((1,)), dma((1,)),
            dma((1,)), dma((1,)),
            dma((8,)), dma((8,)),
            dma((2,)), dma((2,)),
            dma((2,)), dma((2,)),
            dma((2,)), dma((2,)),
            dma((2,)), dma((2,)),
            dma((2,)), dma((2,)),
            dma((1,)), dma((1,)),
        ],
        compiler_params=pltpu.CompilerParams(
            collective_id=0, has_side_effects=True, vmem_limit_bytes=VLIM
        ),
        cost_estimate=pl.CostEstimate(flops=6 * 256 * 1024 * 512, bytes_accessed=4 << 20, transcendentals=0),
    )(
        *(
            pltpu.with_memory_space_constraint(v, pltpu.HBM)
            for v in (
                acts,
                mean_vec.reshape(1, D),
                left_factor,
                right_factor,
                labels.reshape(1, TOK),
            )
        ),
        counts,
    )
    erased, scores, cnt = pl.pallas_call(
        hand_out,
        out_shape=shapes,
        in_specs=[vm] * 3,
        out_specs=(hbm,) * 3,
        scratch_shapes=[dma((3,))],
    )(*(pltpu.with_memory_space_constraint(v, pltpu.VMEM) for v in results))
    return erased, scores, cnt.reshape(RD)


def solution(mesh):
    return jax.shard_map(
        per_device,
        mesh=mesh,
        in_specs=(
            P("dp", "tensor"),
            P("tensor"),
            P("dp", "tensor"),
            P("dp", "tensor"),
            P("dp"),
            P("dp"),
        ),
        out_specs=(P("dp", "tensor"), P("dp", "tensor"), P("dp")),
        check_vma=False,
    )
```

```python
import functools

import jax
import jax.numpy as jnp
from jax import lax
from jax.experimental import pallas as pl
from jax.experimental.pallas import tpu as pltpu
from jax.sharding import PartitionSpec as P

MESH = pl.DeviceIdType.MESH
F32, BF16, I32 = jnp.float32, jnp.bfloat16, jnp.int32
C = 512
NZ, NX, NY = 8, 4, 8
ZORD = (0, 1, 7, 2, 6, 3, 5, 4)
XORD = (0, 1, 3, 2)
ZBACK = tuple(ZORD.index((NZ - d) % NZ) for d in ZORD)
XBACK = tuple(XORD.index((NX - d) % NX) for d in XORD)
NEAR, FAR = (1, 2, 3, 4, 5, 6, 7), (7, 6, 5, 4, 3, 2, 1)
XFIRST = (2, 3, 1)
GROUPS = ((0, 2), (2, 2), (4, 2), (6, 2))
TOK, D, RD = 256, 1024, 8
T2, H, K2 = 512, 512, 128
M = 2 * RD
XW, ZW = 384, 128
YB = T2 // NY
VLIM = 40 << 20
PIECES = 4


def kernel(
    acts, mean, left, right, labels, counts,
    out, scores, cnt,
    meanv, labv, cntv, actv, cen, rg, lg, lo, lm, lab, labo, pbuf, prx, obuf, cbuf, oh, er,
    sxs, sxr, s0, txs, txr, szs, szr, tzs, tzr, fzs, fzr, f0, fxs, fxr, mh, rall, gy, gx, cnts,
    loc, rzs, rzr, rxs, rxr, lzs, lzr, lxs, lxr, bzs, bzr, bxs, bxr, exs, exr,
    pss, psr, css, csr, xxs, xxr, zzs, zzr, ffs, ffr, ggs, ggr,
):
    dp, y = lax.axis_index("dp"), lax.axis_index("tensor")
    c, x, z = lax.rem(dp, 2), lax.rem(dp // 2, NX), dp // (2 * NX)
    oc = 1 - c

    def dev(dz=0, dx=0, dy=0, core=None):
        core = c if core is None else core
        zz, xx, yy = lax.rem(z + dz, NZ), lax.rem(x + dx, NX), lax.rem(y + dy, NY)
        return ((zz * NX + xx) * 2 + core, yy)

    other = dev(core=oc)

    def send(src, dst, ss, rs, to):
        pltpu.make_async_remote_copy(
            src_ref=src,
            dst_ref=dst,
            send_sem=ss[0].at[ss[1]],
            recv_sem=rs[0].at[rs[1]],
            device_id=to,
            device_id_type=MESH,
        ).start()

    def got(ref, rs):
        sem = rs[0].at[rs[1]]
        pltpu.make_async_remote_copy(
            src_ref=ref, dst_ref=ref, send_sem=sem, recv_sem=sem, device_id=other, device_id_type=MESH
        ).wait_recv()

    def gone(ref, ss):
        sem = ss[0].at[ss[1]]
        pltpu.make_async_remote_copy(
            src_ref=ref, dst_ref=ref, send_sem=sem, recv_sem=sem, device_id=other, device_id_type=MESH
        ).wait_send()

    def along_z(order, src, dst, ss, rs):
        for s in order:
            send(src(s), dst(ZBACK[s]), ss, rs(ZBACK[s]), dev(dz=ZORD[s]))

    def along_y(order, src, dst, ss, rs):
        for s in order:
            send(src(s), dst(ZBACK[s]), ss, rs(ZBACK[s]), dev(dy=ZORD[s]))

    def along_x(src, dst, ss, rs):
        for s in XFIRST:
            send(src(s), dst(XBACK[s]), ss, rs(XBACK[s]), dev(dx=XORD[s]))

    mine, theirs = pl.ds(0, TOK), pl.ds(TOK, TOK)
    loads = [
        pltpu.make_async_copy(src, dst, loc.at[i])
        for i, (src, dst) in enumerate(
            (
                (right, rg.at[0, 0]),
                (acts, actv.at[mine]),
                (mean, meanv),
                (labels, labv),
                (counts, cntv),
                (left, lg.at[0, 0]),
            )
        )
    ]
    for cp in loads:
        cp.start()

    barrier = pltpu.get_barrier_semaphore()
    peers = [dev(dz=ZORD[s]) for s in FAR] + [dev(dy=ZORD[s]) for s in FAR]
    peers += [dev(dx=d) for d in (2, 1, 3)] + [other]
    for p in peers:
        pl.semaphore_signal(barrier, inc=1, device_id=p, device_id_type=MESH)
    loads[0].wait()
    pl.semaphore_wait(barrier, len(peers))

    group_of = {s: g for g, (first, number) in enumerate(GROUPS) for s in range(first, first + number)}
    along_z(NEAR, lambda s: rg.at[0, 0], lambda t: rg.at[0, t], (rzs, 0), lambda t: (rzr, group_of[t]))
    loads[1].wait()
    send(actv.at[mine], actv.at[theirs], (exs, 0), (exr, 0), other)
    for cp in loads[2:]:
        cp.wait()
    cen[mine, :] = (actv[mine, :].astype(F32) - meanv[...]).astype(BF16)
    slot_iota = lax.broadcasted_iota(I32, (1, TOK), 1)
    lab[0, 0, 0] = jnp.where(slot_iota < cntv[0], labv[...], -1)
    send(lab.at[0, 0, 0], labo, (exs, 5), (exr, 5), other)

    def right_x(g):
        first, number = GROUPS[g]
        got(rg.at[0, max(first, 1) : first + number], (rzr, g))
        zs = pl.ds(first, number)
        along_x(lambda s: rg.at[0, zs], lambda t: rg.at[t, zs], (rxs, 0), lambda t: (rxr, first // 4))

    half, their_half = pl.ds(pl.multiple_of(c * H, H), H), pl.ds(pl.multiple_of(oc * H, H), H)
    right_x(0)
    right_x(1)
    got(labo, (exr, 5))
    tokens = jnp.concatenate([lab[0, 0, 0], labo[...]], axis=1)
    for xs in range(NX):
        for zs in range(NZ):
            r = lax.broadcasted_iota(I32, (2 * RD, T2), 0)
            owner = lax.rem(z + ZORD[zs], NZ) * NX + lax.rem(x + XORD[xs], NX)
            at = (xs * NZ + zs) * 2 * RD
            oh[at : at + 2 * RD, :] = (owner * (2 * RD) + r == tokens).astype(F32).astype(BF16)
    own_sums = jnp.dot(oh[:, 0:TOK], actv[mine, half], preferred_element_type=F32)
    got(actv.at[theirs], (exr, 0))
    sums = own_sums + jnp.dot(oh[:, TOK:T2], actv[theirs, half], preferred_element_type=F32)
    for zs in range(NZ):
        for xs in range(NX):
            at = (xs * NZ + zs) * M
            part = sums[at : at + M, XW:]
            if zs:
                fzs[zs, xs * M : (xs + 1) * M, :] = part.astype(BF16)
            else:
                f0[xs * M : (xs + 1) * M, :] = part
    along_z(NEAR, lambda s: fzs.at[s], lambda t: fzr.at[t], (ffs, 0), lambda t: (ffr, 0))
    s0[...] = sums[:128, :XW]
    txs[...] = jnp.sum(sums, axis=0, keepdims=True)
    for s in range(1, NX):
        sxs[s] = sums[s * 128 : (s + 1) * 128, :XW].astype(BF16)
    along_x(lambda s: sxs.at[s], lambda t: sxr.at[t], (xxs, 0), lambda t: (xxr, 0))
    along_x(lambda s: txs, lambda t: txr.at[t], (xxs, 1), lambda t: (xxr, 1))
    right_x(2)
    right_x(3)
    cen[theirs, :] = (actv[theirs, :].astype(F32) - meanv[...]).astype(BF16)
    along_z(NEAR, lambda s: lab.at[0, 0, 0], lambda t: lab.at[0, 0, t], (bzs, 0), lambda t: (bzr, 0))

    def block(s):
        return pl.ds(pl.multiple_of(lax.rem(y + ZORD[s], NY) * YB, YB), YB)

    def chunk(k):
        got(rg.at[1:NX, 4 * k : 4 * k + 4], (rxr, k))
        rmat = rg[:, 4 * k : 4 * k + 4].astype(F32).reshape(K2, D).astype(BF16)
        rall[k * K2 : (k + 1) * K2, :] = rmat
        part = lax.dot_general(cen[...], rmat, (((1,), (1,)), ((), ())), preferred_element_type=F32)
        pbuf[k] = part.astype(BF16)
        along_y(FAR, lambda s: pbuf.at[k, block(s)], lambda t: prx.at[k, t], (pss, k), lambda t: (psr, k))

    near_half = y < NY // 2
    taker = lax.rem(c + y // (NY // 2), 2)

    def reduce(k):
        total = pbuf[k, block(0), :].astype(F32)
        got(prx.at[k, 1:NY], (psr, k))
        for s in range(1, NY):
            total = total + prx[k, s].astype(F32)
        obuf[k] = total.astype(BF16)
        there = cbuf.at[k, block(0)]
        for s in FAR:
            send(obuf.at[k], there, (css, k), (csr, k), dev(dy=ZORD[s], core=taker))

        @pl.when(near_half)
        def _():
            there[...] = obuf[k]

        @pl.when(jnp.logical_not(near_half))
        def _():
            send(obuf.at[k], there, (css, k), (csr, k), other)

    def gathered(k):
        @pl.when(near_half)
        def _():
            got(cbuf.at[k, 0 : T2 - YB], (csr, k))

        @pl.when(jnp.logical_not(near_half))
        def _():
            got(cbuf.at[k], (csr, k))

    along_z(NEAR, lambda s: lg.at[0, 0], lambda t: lg.at[0, t], (lzs, 0), lambda t: (lzr, 0))
    chunk(0)
    got(lab.at[0, 0, 1:NZ], (bzr, 0))
    along_x(lambda s: lab.at[0, 0], lambda t: lab.at[0, t], (bxs, 0), lambda t: (bxr, 0))
    chunk(1)
    got(lg.at[0, 1:NZ], (lzr, 0))
    along_x(lambda s: lg.at[0], lambda t: lg.at[t], (lxs, 0), lambda t: (lxr, 0))
    got(lab.at[0, 1:NX], (bxr, 0))
    send(lab.at[0], lab.at[1], (exs, 1), (exr, 1), other)

    total = s0[...]
    got(sxr.at[1:NX], (xxr, 0))
    for s in range(1, NX):
        total = total + sxr[s].astype(F32)
    for s in NEAR:
        szs[s] = total[s * 2 * RD : (s + 1) * 2 * RD, :].astype(BF16)
    mh[0, :, 0:XW] = total[0:M]
    along_z(FAR, lambda s: szs.at[s], lambda t: szr.at[t], (zzs, 0), lambda t: (zzr, 0))
    total = txs[...]
    got(txr.at[1:NX], (xxr, 1))
    for s in range(1, NX):
        total = total + txr[s]
    tzs[...] = total
    along_z(FAR, lambda s: tzs, lambda t: tzr.at[t], (zzs, 1), lambda t: (zzr, 1))
    total = f0[...]
    got(fzr.at[1:NZ], (ffr, 0))
    for s in range(1, NZ):
        total = total + fzr[s].astype(F32)
    mh[0, :, XW:] = total[0:M]
    for s in range(1, NX):
        fxs[s] = total[s * M : (s + 1) * M, :].astype(BF16)
    along_x(lambda s: fxs.at[s], lambda t: fxr.at[t], (ffs, 1), lambda t: (ffr, 1))
    reduce(0)
    reduce(1)

    got(lab.at[1], (exr, 1))
    chip = z * NX + x
    own_class = chip * (2 * RD) + lax.broadcasted_iota(I32, (2 * RD, TOK), 0)
    hits, valid = jnp.zeros((2 * RD, TOK), F32), jnp.zeros((1, TOK), F32)
    for k in range(2):
        for xs in range(NX):
            for zs in range(NZ):
                row = lab[k, xs, zs]
                hits = hits + (row == own_class).astype(F32)
                valid = valid + (row >= 0).astype(F32)
    own_counts = jnp.sum(hits, axis=1, keepdims=True)
    grand = jnp.sum(valid, axis=1, keepdims=True)

    got(szr.at[1:NZ], (zzr, 0))
    got(tzr.at[1:NZ], (zzr, 1))
    first_sums, other_sums, total = mh[0, :, 0:XW], mh[0, :, XW:], tzs[...]
    for s in range(1, NZ):
        first_sums = first_sums + szr[s].astype(F32)
        total = total + tzr[s]
    got(fxr.at[1:NX], (ffr, 1))
    for s in range(1, NX):
        other_sums = other_sums + fxr[s].astype(F32)
    mean_act = total / grand
    mh[0, :, 0:XW] = first_sums - own_counts * mean_act[:, 0:XW]
    mh[0, :, XW:] = other_sums - own_counts * mean_act[:, XW:]
    send(mh.at[0], mh.at[1], (exs, 6), (exr, 6), other)

    def twice(a, b, dims):
        high = a.astype(BF16).astype(F32)
        terms = jnp.concatenate([high, a - high], axis=0).astype(BF16)
        both = lax.dot_general(terms, b, (dims, ((), ())), preferred_element_type=F32)
        return both[: a.shape[0]] + both[a.shape[0] :]

    got(mh.at[1], (exr, 6))
    gsum = twice(mh[0], rall[:, half], ((1,), (1,))) + twice(mh[1], rall[:, their_half], ((1,), (1,)))
    gy[0] = gsum.astype(BF16)
    along_y(FAR, lambda s: gy.at[0], lambda t: gy.at[t], (ggs, 0), lambda t: (ggr, 0))

    got(lg.at[1:NX], (lxr, 0))
    send(lg, lo, (exs, 2), (exr, 2), other)
    for k in range(2):
        lm[k * K2 : (k + 1) * K2, :] = lg[:, 4 * k : 4 * k + 4].astype(F32).reshape(K2, D).astype(BF16)
    got(lo, (exr, 2))
    for k in range(2, 4):
        lm[k * K2 : (k + 1) * K2, :] = lo[:, 4 * k - 8 : 4 * k - 4].astype(F32).reshape(K2, D).astype(BF16)
    gathered(0)
    gathered(1)

    coords = jnp.concatenate([cbuf[0, 0:TOK], cbuf[1, 0:TOK], cbuf[0, TOK:T2], cbuf[1, TOK:T2]], axis=1)
    keeps = []
    for q in range(2):
        cols = pl.ds(q * H, H)
        corr = jnp.dot(coords, lm[:, cols], preferred_element_type=F32)
        er[:, cols] = (actv[mine, cols].astype(F32) - corr).astype(BF16)
        keeps.append(pltpu.make_async_copy(er.at[:, cols], out.at[:, cols], loc.at[6 + q]))
        keeps[q].start()

    got(gy.at[1:NY], (ggr, 0))
    for s in range(1, NY):
        gsum = gsum + gy[s].astype(F32)
    gx[0] = gsum
    ours, others = pl.ds(pl.multiple_of(c * RD, RD), RD), pl.ds(pl.multiple_of(oc * RD, RD), RD)
    send(gx.at[0, others], gx.at[1, others], (exs, 7), (exr, 7), other)
    cnts[...] = jnp.broadcast_to(own_counts, (M, 128))
    own_counts = cnts[ours, 0:1]
    lane = lax.broadcasted_iota(I32, (RD, RD), 1)
    row = lax.broadcasted_iota(I32, (RD, RD), 0)
    cnt[...] = jnp.sum(jnp.where(lane == row, own_counts, 0.0), axis=0, keepdims=True).astype(I32)
    scale = 1.0 / jnp.sqrt(jnp.maximum(own_counts, 1.0))
    got(gx.at[1, ours], (exr, 7))
    coords = jnp.concatenate([gx[0, ours, :], gx[1, ours, :]], axis=1)
    moved = twice(coords, lm[...], ((1,), (0,)))
    scores[...] = moved * -scale
    for k, cols in enumerate((half, their_half)):
        scores[:, cols] += mh[k, ours, :] * scale

    for cp in keeps:
        cp.wait()
    gone(rg.at[0, 1:NZ], (rzs, 0))
    gone(rg.at[1:NX], (rxs, 0))
    gone(lab.at[0, 0, 1:NZ], (bzs, 0))
    gone(lg.at[0, 1:NZ], (lzs, 0))
    gone(lab.at[0, 1:NX], (bxs, 0))
    gone(lg.at[1:NX], (lxs, 0))
    gone(actv.at[mine], (exs, 0))
    gone(lab.at[0], (exs, 1))
    gone(lo, (exs, 2))
    for k in range(2):
        gone(prx.at[k, 1:NY], (pss, k))
    gone(sxr.at[1:NX], (xxs, 0))
    gone(szr.at[1:NZ], (zzs, 0))
    gone(txr.at[1:NX], (xxs, 1))
    gone(tzr.at[1:NZ], (zzs, 1))

    @pl.when(near_half)
    def _():
        for k in range(2):
            gone(cbuf.at[k, 0 : T2 - YB], (css, k))

    @pl.when(jnp.logical_not(near_half))
    def _():
        for k in range(2):
            gone(cbuf.at[k], (css, k))

    gone(fzr.at[1:NZ], (ffs, 0))
    gone(fxr.at[1:NX], (ffs, 1))
    gone(gy.at[1:NY], (ggs, 0))
    gone(labo, (exs, 5))
    gone(mh.at[0], (exs, 6))
    gone(gx.at[0, others], (exs, 7))


def hand_out(erased, scores, cnt, erased_out, scores_out, cnt_out, sems):
    pairs = ((erased, erased_out), (scores, scores_out), (cnt, cnt_out))
    copies = [pltpu.make_async_copy(a, b, sems.at[i]) for i, (a, b) in enumerate(pairs)]
    for cp in copies:
        cp.start()
    for cp in copies:
        cp.wait()


def per_device(acts, mean_vec, left_factor, right_factor, labels, counts):
    dma = pltpu.SemaphoreType.DMA
    ng = len(GROUPS)
    vm, anywhere = pl.BlockSpec(memory_space=pltpu.VMEM), pl.BlockSpec(memory_space=pl.ANY)
    hbm = pl.BlockSpec(memory_space=pltpu.HBM)
    shapes = (
        jax.ShapeDtypeStruct((TOK, D), BF16),
        jax.ShapeDtypeStruct((RD, D), F32),
        jax.ShapeDtypeStruct((1, RD), I32),
    )
    results = pl.pallas_call(
        kernel,
        out_shape=tuple(pltpu.VMEM(v.shape, v.dtype) for v in shapes),
        in_specs=[hbm] * 6,
        scratch_shapes=[
            pltpu.VMEM((1, D), F32),
            pltpu.VMEM((1, TOK), I32),
            pltpu.SMEM((1,), I32),
            pltpu.VMEM((T2, D), BF16),
            pltpu.VMEM((T2, D), BF16),
            pltpu.VMEM((NX, NZ, RD, D), BF16),
            pltpu.VMEM((NX, NZ, RD, D), BF16),
            pltpu.VMEM((NX, NZ, RD, D), BF16),
            pltpu.VMEM((C, D), BF16),
            pltpu.VMEM((2, NX, NZ, 1, TOK), I32),
            pltpu.VMEM((1, TOK), I32),
            pltpu.VMEM((2, T2, K2), BF16),
            pltpu.VMEM((2, NY, YB, K2), BF16),
            pltpu.VMEM((2, YB, K2), BF16),
            pltpu.VMEM((2, T2, K2), BF16),
            pltpu.VMEM((C, T2), BF16),
            pltpu.VMEM((TOK, D), BF16),
            pltpu.VMEM((NX, 128, XW), BF16),
            pltpu.VMEM((NX, 128, XW), BF16),
            pltpu.VMEM((128, XW), F32),
            pltpu.VMEM((1, H), F32),
            pltpu.VMEM((NX, 1, H), F32),
            pltpu.VMEM((NZ, M, XW), BF16),
            pltpu.VMEM((NZ, M, XW), BF16),
            pltpu.VMEM((1, H), F32),
            pltpu.VMEM((NZ, 1, H), F32),
            pltpu.VMEM((NZ, NX * M, ZW), BF16),
            pltpu.VMEM((NZ, NX * M, ZW), BF16),
            pltpu.VMEM((NX * M, ZW), F32),
            pltpu.VMEM((NX, M, ZW), BF16),
            pltpu.VMEM((NX, M, ZW), BF16),
            pltpu.VMEM((2, M, H), F32),
            pltpu.VMEM((256, D), BF16),
            pltpu.VMEM((NY, M, 256), BF16),
            pltpu.VMEM((2, M, 256), F32),
            pltpu.VMEM((M, 128), F32),
            dma((8,)),
            dma((1,)), dma((ng,)),
            dma((1,)), dma((2,)),
            dma((1,)), dma((1,)),
            dma((1,)), dma((1,)),
            dma((1,)), dma((1,)),
            dma((1,)), dma((1,)),
            dma((8,)), dma((8,)),
            dma((2,)), dma((2,)),
            dma((2,)), dma((2,)),
            dma((2,)), dma((2,)),
            dma((2,)), dma((2,)),
            dma((2,)), dma((2,)),
            dma((1,)), dma((1,)),
        ],
        compiler_params=pltpu.CompilerParams(
            collective_id=0, has_side_effects=True, vmem_limit_bytes=VLIM
        ),
        cost_estimate=pl.CostEstimate(flops=6 * 256 * 1024 * 512, bytes_accessed=4 << 20, transcendentals=0),
    )(
        *(
            pltpu.with_memory_space_constraint(v, pltpu.HBM)
            for v in (
                acts,
                mean_vec.reshape(1, D),
                left_factor,
                right_factor,
                labels.reshape(1, TOK),
            )
        ),
        counts,
    )
    erased, scores, cnt = pl.pallas_call(
        hand_out,
        out_shape=shapes,
        in_specs=[vm] * 3,
        out_specs=(hbm,) * 3,
        scratch_shapes=[dma((3,))],
    )(*(pltpu.with_memory_space_constraint(v, pltpu.VMEM) for v in results))
    return erased, scores, cnt.reshape(RD)


def solution(mesh):
    return jax.shard_map(
        per_device,
        mesh=mesh,
        in_specs=(
            P("dp", "tensor"),
            P("tensor"),
            P("dp", "tensor"),
            P("dp", "tensor"),
            P("dp"),
            P("dp"),
        ),
        out_specs=(P("dp", "tensor"), P("dp", "tensor"), P("dp")),
        check_vma=False,
    )
```
